128 devices in a mesh: section: 4 (over x), dp: 4 (over y), mp: 8 (over z, core).
Axes of the slice: x: 4, y: 4, z: 4, core: 2. Of those that a mesh axis runs over, the one named last changes fastest.
Arguments:
- patches: bfloat16 [1024, 5120], P('dp'), may hold values from -6 to 6
- ln_gain: float32 [1280], replicated, may hold values from 0.25 to 1.75
- ln_bias: float32 [1280], replicated, may hold values from -3 to 3
- w_merge_in: bfloat16 [5120, 5120], P(None, ('section', 'mp')), may hold values from -0.078125 to 0.078125
- b_merge_in: float32 [5120], P(('section', 'mp')), may hold values from -3 to 3
- w_merge_out: bfloat16 [5120, 8192], P(('section', 'mp')), may hold values from -0.15625 to 0.15625
- b_merge_out: float32 [8192], replicated, may hold values from -3 to 3
- text_rows: bfloat16 [4, 4, 128, 8192], P('section', 'dp', None, 'mp'), may hold values from -6 to 6
- section_gain: float32 [4, 8192], P('section'), may hold values from 0.1 to 1.9
- section_weight: bfloat16 [4, 8192, 8192], P('section', None, 'mp'), may hold values from -0.0625 to 0.0625
- image_sizes: int32 [4, 64], replicated, may hold values from 1 to 8, 256 in all within a row
- placement: int32 [4, 64], replicated, may hold values from 0 to 63, each once within a row
- offsets: int32 [4, 64], replicated, may hold values from 0 to 7
Outputs:
- final_stream: bfloat16 [4, 4, 128, 8192], P('section', 'dp', None, 'mp')
The draws below stay inside these ranges and needn't reach their ends.
Inputs may be any that keep to these rules, and one draw needn't show every extreme that they name: `image_sizes`: each row sums to 256; the largest entry is exactly 8. `placement`: each row is a permutation, so each encoder group sends exactly 4 images to every owner.
All inputs are finite; a program needn't handle non-finite values.
Results may differ from the reference program's by a relative error of at most 0.02.
Values may be sent and summed in bfloat16 or wider, within the bound.
A program may use at most 128 MiB of HBM per device.

```python
import math
import jax
import jax.numpy as jnp
import numpy as np
from jax import lax

D = 8192
VD = 1280
MH = 5120
SLOT = 8
K_PAIR = 4
MI = 5120
IMG_ENC = 64
E_ROWS = 256
L = 128
MICRO = 4
SEQS = 4
N_SECTION = 4
N_DP = 4
N_MP = 8


def plant(result, stream_key, least, high):
    dims = result.shape
    spot = [jax.random.randint(jax.random.fold_in(stream_key, axis), (), 0, dims[axis]) for axis in range(len(dims))]
    result = result.at[tuple(spot)].set(least)
    longest = dims.index(max(dims))
    spot[longest] = (spot[longest] + 1) % dims[longest]
    return result.at[tuple(spot)].set(high)


def strengthened(drawn, own_key, source, target, parts, factor):
    def block_of(axis_at):
        return (jnp.arange(drawn.shape[axis_at]) // (drawn.shape[axis_at] // parts)).reshape((-1,) + (1,) * (drawn.ndim - 1 - axis_at))

    one_side = jax.random.permutation(own_key, parts)[block_of(target)]
    second = (block_of(target) + parts // 2) % parts
    return jnp.where((block_of(source) == one_side) | (block_of(source) == second), factor * drawn, drawn)


def block_scale(key, shape, split, least, largest):
    loudness = 1.0
    for dim, parts in split:
        steps = jax.random.uniform(jax.random.fold_in(jax.random.fold_in(key, 6), dim), (parts,), jnp.float32, least / len(split), largest / len(split))
        loudness = loudness * jnp.repeat(jnp.exp(steps), shape[dim] // parts).reshape((-1,) + (1,) * (len(shape) - 1 - dim))
    return loudness


def split_up(count, total, bound, skew):
    weights = [(1 << 20) // math.isqrt(rank ** skew) + 1 for rank in range(2, count + 1)]
    surplus, holding = total - bound - (count - 1), [1] * (count - 1)
    while surplus > 0:
        movable = [i for i in range(count - 1) if holding[i] < bound]
        whole, left = sum([weights[i] for i in movable]), surplus
        for i in movable:
            more = min(bound - holding[i], max(1, left * weights[i] // whole), surplus)
            holding[i] = holding[i] + more
            surplus = surplus - more
    return np.array([bound] + holding)


def ragged(own_key, count, total, bound, skew):
    if count == 2:
        one = jax.random.randint(own_key, (), max(1, total - bound), min(bound, total - 1) + 1)
        return jnp.stack([one, total - one])
    tallies = jnp.asarray(split_up(count, total, bound, skew), jnp.int32)
    pairs = (count - 1) // 2
    donor, receiver = tallies[1:1 + 2 * pairs:2], tallies[2:2 + 2 * pairs:2]
    margin = jnp.minimum(donor - 1, bound - receiver)
    shifted = jax.random.randint(jax.random.fold_in(own_key, 1), (pairs,), 0, 1 << 20) % (margin + 1)
    tallies = tallies.at[1:1 + 2 * pairs:2].set(donor - shifted).at[2:2 + 2 * pairs:2].set(receiver + shifted)
    return tallies[jax.random.permutation(jax.random.fold_in(own_key, 2), count)]


def gaussian(stream_key, shape, scale, bound, shards=(), kind=jnp.bfloat16):
    values = scale * jax.random.normal(stream_key, shape, jnp.float32)
    if shards:
        values = values * block_scale(stream_key, shape, shards, -0.22, 0.18)
    return jnp.clip(values, -bound, bound).astype(kind)


def bell_draw_with(rng, shape, scale, limit, cuts, heavy, kind=jnp.bfloat16):
    values = scale * jax.random.normal(rng, shape, jnp.float32)
    if cuts:
        values = values * block_scale(rng, shape, cuts, -0.22, 0.18)
    return jnp.clip(strengthened(values, jax.random.fold_in(rng, 3), *heavy), -limit, limit).astype(kind)


def setup_inputs(seed: int = 0) -> dict:
    arg_keys = jax.random.split(jax.random.key(seed), 14)
    patches = gaussian(arg_keys[0], (N_DP * E_ROWS, MI), 1.0, 6.0, ((0, 4),))
    ln_gain = jnp.clip(1.0 + 0.15 * jax.random.normal(arg_keys[1], (VD,), jnp.float32), 0.25, 1.75)
    ln_bias = gaussian(arg_keys[2], (VD,), 0.5, 3.0, (), jnp.float32)
    w_merge_in = gaussian(arg_keys[3], (MI, MH), MI ** -0.5, 0.078125, ((1, 32),))
    b_merge_in = gaussian(arg_keys[4], (MH,), 0.5, 3.0, ((0, 32),), jnp.float32)
    w_merge_out = bell_draw_with(arg_keys[5], (MH, D), MH ** -0.5, 0.15625, ((0, 32),), (0, 1, 32, 2.75))
    b_merge_out = gaussian(arg_keys[6], (D,), 0.5, 3.0, (), jnp.float32)
    text_rows = gaussian(arg_keys[7], (MICRO, SEQS, L, D), 1.0, 6.0, ((0, 4), (1, 4), (3, 8)))
    section_gain = jnp.clip(1.0 + 0.18 * jax.random.normal(arg_keys[8], (MICRO, D), jnp.float32), 0.1, 1.9)
    section_weight = gaussian(arg_keys[9], (MICRO, D, D), D ** -0.5, 0.0625, ((0, 4), (2, 8)))
    image_sizes = jax.vmap(lambda own: ragged(own, IMG_ENC, E_ROWS, SLOT, 1))(jax.random.split(arg_keys[10], N_DP)).reshape((N_DP, IMG_ENC)).astype(jnp.int32)
    placement = jax.vmap(lambda own: jax.random.permutation(own, IMG_ENC))(jax.random.split(arg_keys[11], N_DP)).reshape((N_DP, IMG_ENC)).astype(jnp.int32)
    offsets = plant(jax.random.randint(arg_keys[12], (N_DP, IMG_ENC), 0, SLOT), jax.random.fold_in(arg_keys[12], 1), 0, SLOT - 1).astype(jnp.int32)
    return dict(patches=patches, ln_gain=ln_gain, ln_bias=ln_bias, w_merge_in=w_merge_in, b_merge_in=b_merge_in, w_merge_out=w_merge_out, b_merge_out=b_merge_out, text_rows=text_rows, section_gain=section_gain, section_weight=section_weight, image_sizes=image_sizes, placement=placement, offsets=offsets)


def slot_layout(image_sizes, placement, offsets, owners, k_pair, slot_len, rows_enc):
    targets = owners[:, None] * k_pair + jnp.arange(k_pair, dtype=jnp.int32)[None, :]
    matches = placement[:, None, None, :] == targets[None, :, :, None]
    starts = jnp.cumsum(image_sizes, axis=1) - image_sizes

    def picker(values):
        return lax.optimization_barrier(jnp.sum(jnp.where(matches, values[:, None, None, :], 0), axis=-1)).astype(jnp.int32)
    extent = picker(image_sizes)
    first_row = picker(starts)
    shift_in = jnp.minimum(picker(offsets), slot_len - extent)
    column = jnp.arange(slot_len, dtype=jnp.int32)
    inside = (column >= shift_in[..., None]) & (column < (shift_in + extent)[..., None])
    source = jnp.clip(first_row[..., None] + column - shift_in[..., None], 0, rows_enc - 1).astype(jnp.int32)
    return (source, inside)

def layer_norm(patches, ln_gain, ln_bias):
    values = patches.astype(jnp.float32).reshape(patches.shape[0], 4, -1)
    centre = values - lax.optimization_barrier(jnp.mean(values, axis=-1, keepdims=True))
    spread = lax.optimization_barrier(jnp.mean(centre * centre, axis=-1, keepdims=True))
    normed = centre * lax.rsqrt(spread + 1e-06) * ln_gain + ln_bias
    return normed.reshape(patches.shape[0], -1).astype(jnp.bfloat16)

def reference(patches, ln_gain, ln_bias, w_merge_in, b_merge_in, w_merge_out, b_merge_out, text_rows, section_gain, section_weight, image_sizes, placement, offsets):
    encoded = layer_norm(patches, ln_gain, ln_bias)
    hidden = jax.nn.gelu(jnp.dot(encoded, w_merge_in, preferred_element_type=jnp.float32) + b_merge_in, approximate=False).astype(jnp.bfloat16)
    blocks = N_SECTION * N_MP
    block_width = MH // blocks

    def add_block(running, block_idx):
        hidden_part = lax.dynamic_slice_in_dim(hidden, block_idx * block_width, block_width, 1)
        weight_rows = lax.dynamic_slice_in_dim(w_merge_out, block_idx * block_width, block_width, 0)
        term = lax.optimization_barrier(jnp.dot(hidden_part, weight_rows, preferred_element_type=jnp.float32).astype(jnp.bfloat16))
        return (running + term.astype(jnp.float32), None)
    running, unused = lax.scan(add_block, jnp.zeros((hidden.shape[0], D), jnp.float32), jnp.arange(blocks, dtype=jnp.int32))
    merged = (running + b_merge_out).astype(jnp.bfloat16)
    owners = jnp.arange(N_SECTION * N_DP, dtype=jnp.int32)
    source, inside = slot_layout(image_sizes, placement, offsets, owners, K_PAIR, SLOT, E_ROWS)
    source = source + (jnp.arange(N_DP, dtype=jnp.int32) * E_ROWS)[:, None, None, None]
    source = jnp.transpose(source, (1, 0, 2, 3)).reshape(N_SECTION * N_DP, L)
    inside = jnp.transpose(inside, (1, 0, 2, 3)).reshape(N_SECTION * N_DP, L)
    image_part = merged[source]
    stream = jnp.where(inside[..., None], image_part, text_rows.reshape(N_SECTION * N_DP, L, D))
    for layer_idx in range(N_SECTION):
        values = stream.astype(jnp.float32)
        square = lax.optimization_barrier(jnp.mean(values * values, axis=-1, keepdims=True))
        normed = (values * lax.rsqrt(square + 1e-06) * section_gain[layer_idx]).astype(jnp.bfloat16)
        update = jnp.dot(normed.reshape(-1, D), section_weight[layer_idx], preferred_element_type=jnp.float32).reshape(values.shape)
        stream = (values + update).astype(jnp.bfloat16)
    return stream.reshape(MICRO, SEQS, L, D)
```

```python
import jax
import jax.numpy as jnp
from jax import lax
from jax.experimental import pallas as pl
from jax.experimental.pallas import tpu as pltpu
from jax.sharding import PartitionSpec as P

SLOT = 8
K_PAIR = 4
ROWS = 64
MESH = pl.DeviceIdType.MESH


def slot_layout(image_sizes, placement, offsets, owners, k_pair, slot_len, rows_enc):
    targets = owners[:, None] * k_pair + jnp.arange(k_pair, dtype=jnp.int32)[None, :]
    matches = placement[:, None, None, :] == targets[None, :, :, None]
    count = image_sizes.shape[1]
    earlier = jnp.arange(count)[:, None] < jnp.arange(count)[None, :]
    starts = jnp.sum(jnp.where(earlier[None], image_sizes[:, :, None], 0), axis=1)

    def picker(values):
        return jnp.sum(jnp.where(matches, values[:, None, None, :], 0), axis=-1)

    extent = picker(image_sizes)
    first_row = picker(starts)
    shift_in = jnp.minimum(picker(offsets), slot_len - extent)
    column = jnp.arange(slot_len, dtype=jnp.int32)
    inside = (column >= shift_in[..., None]) & (column < (shift_in + extent)[..., None])
    source = jnp.clip(first_row[..., None] + column - shift_in[..., None], 0, rows_enc - 1)
    return (source, inside)


def layer_norm(patches, ln_gain, ln_bias):
    values = patches.astype(jnp.float32).reshape(patches.shape[0], 4, -1)
    centre = values - jnp.mean(values, axis=-1, keepdims=True)
    spread = jnp.mean(centre * centre, axis=-1, keepdims=True)
    normed = centre * lax.rsqrt(spread + 1e-06) * ln_gain + ln_bias
    return normed.reshape(patches.shape[0], -1).astype(jnp.bfloat16)


def layers_kernel(
    stream_ref, gain_ref, weight_hbm, out_ref,
    shards, weight, total, squares, results,
    weight_sem, got, sent, home_sem, gone_sem,
):
    section = lax.axis_index("section")
    mp = lax.axis_index("mp")
    n_section = lax.axis_size("section")
    n_mp = lax.axis_size("mp")
    n_ring = n_mp // 2
    chip, core = mp // 2, lax.rem(mp, 2)
    chunks, _, rows, width = shards.shape
    per_micro = chunks // n_section

    def at(chip_pos, core_pos):
        return lax.rem(chip_pos + n_ring, n_ring) * 2 + core_pos

    ahead, behind = at(chip + 1, core), at(chip - 1, core)
    sibling = at(chip, 1 - core)
    turn = 1 - 2 * core
    onward, source = at(chip + turn, core), at(chip - turn, core)
    far = at(chip + 2, core)

    def shard_copy(t, idx, slot, **target):
        return pltpu.make_async_remote_copy(
            src_ref=shards.at[t, idx], dst_ref=shards.at[t, idx],
            send_sem=sent.at[t, slot], recv_sem=got.at[t, idx],
            device_id=target, device_id_type=MESH,
        )

    def arrival(t, idx):
        shard_copy(t, idx, 0, mp=sibling).wait_recv()

    def load(idx):
        return pltpu.make_async_copy(weight_hbm.at[idx], weight.at[idx], weight_sem.at[idx])

    for idx in range(n_mp):
        load(idx).start()

    barrier = pltpu.get_barrier_semaphore()
    for partner in (ahead, behind, sibling):
        pl.semaphore_signal(barrier, inc=1, device_id={"mp": partner}, device_id_type=MESH)
    for hop in range(1, n_section):
        pl.semaphore_signal(
            barrier, inc=1, device_id={"section": lax.rem(section + hop, n_section)}, device_id_type=MESH
        )
    pl.semaphore_wait(barrier, 2 + n_section)

    def feed(half, t):
        return pltpu.make_async_remote_copy(
            src_ref=stream_ref.at[pl.ds(half * rows, rows)], dst_ref=shards.at[t, mp],
            send_sem=gone_sem.at[half], recv_sem=got.at[t, mp],
            device_id={"section": 0}, device_id_type=MESH,
        )

    for half in range(per_micro):
        @pl.when(section == 0)
        def _():
            pltpu.make_async_copy(
                stream_ref.at[pl.ds(half * rows, rows)], shards.at[half, mp], got.at[half, mp]
            ).start()

        @pl.when(section != 0)
        def _():
            feed(half, section * per_micro + half).start()

    def pass_on(t):
        return pltpu.make_async_remote_copy(
            src_ref=results.at[t], dst_ref=shards.at[t, mp],
            send_sem=sent.at[t, 7], recv_sem=got.at[t, mp],
            device_id={"section": section + 1}, device_id_type=MESH,
        )

    def bring_home(t):
        half = lax.rem(t, per_micro)
        return pltpu.make_async_remote_copy(
            src_ref=results.at[t], dst_ref=out_ref.at[pl.ds(pl.multiple_of(half * rows, rows), rows)],
            send_sem=sent.at[t, 7], recv_sem=home_sem.at[half],
            device_id={"section": t // per_micro}, device_id_type=MESH,
        )

    def add(t, idx):
        values = shards[t, idx].astype(jnp.float32)
        square = values * values
        lanes = squares[...]
        for j in range(0, width, 128):
            lanes = lanes + square[:, j : j + 128]
        squares[...] = lanes
        scaled = (values * gain_ref[pl.ds(idx, 1), :]).astype(jnp.bfloat16)
        total[...] += jnp.dot(scaled, weight[idx], preferred_element_type=jnp.float32)

    last = n_section - 1

    def turn_body(i, carry):
        t = i - 1

        @pl.when(i < chunks)
        def _():
            arrival(i, mp)
            shard_copy(i, mp, 0, mp=onward).start()
            shard_copy(i, mp, 1, mp=source).start()
            shard_copy(i, mp, 2, mp=sibling).start()

        @pl.when(i == 1)
        def _():
            for idx in range(n_mp):
                load(idx).wait()

        @pl.when(i > 0)
        def _():
            total[...] = jnp.zeros_like(total)
            squares[...] = jnp.zeros_like(squares)
            add(t, mp)
            add(t, source)
            add(t, onward)
            arrival(t, far)
            shard_copy(t, far, 3, mp=sibling).start()
            add(t, far)
            for step in (0, 1, -1):
                idx = at(chip + step, 1 - core)
                arrival(t, idx)
                add(t, idx)

        @pl.when(i < chunks)
        def _():
            arrival(i, source)
            shard_copy(i, source, 4, mp=onward).start()
            shard_copy(i, source, 5, mp=sibling).start()
            arrival(i, onward)
            shard_copy(i, onward, 6, mp=sibling).start()

        @pl.when(i > 0)
        def _():
            idx = at(chip + 2, 1 - core)
            arrival(t, idx)
            add(t, idx)
            square = jnp.sum(squares[...], axis=-1, keepdims=True) * (1.0 / (n_mp * width))
            update = total[...] * lax.rsqrt(square + 1e-06)
            result = (shards[t, mp].astype(jnp.float32) + update).astype(jnp.bfloat16)
            results[t] = result

            @pl.when(section < last)
            def _():
                pass_on(t).start()

            @pl.when((section == last) & (t < last * per_micro))
            def _():
                bring_home(t).start()

            @pl.when((section == last) & (t >= last * per_micro))
            def _():
                half = lax.rem(t, per_micro)
                out_ref[pl.ds(pl.multiple_of(half * rows, rows), rows)] = result

        return carry

    lax.fori_loop(0, chunks + 1, turn_body, 0)

    @pl.when(section < last)
    def _():
        for half in range(per_micro):
            bring_home(half).wait_recv()

    def settle(t, carry):
        for slot in range(7):
            shard_copy(t, mp, slot, mp=sibling).wait_send()

        @pl.when((section < last) | (t < last * per_micro))
        def _():
            shard_copy(t, mp, 7, mp=sibling).wait_send()

        return carry

    lax.fori_loop(0, chunks, settle, 0)

    @pl.when(section != 0)
    def _():
        for half in range(per_micro):
            feed(half, half).wait_send()


def layers(stream, gain, weight, n_section, n_mp):
    seq_len, width = stream.shape
    chunks = n_section * seq_len // ROWS
    return pl.pallas_call(
        layers_kernel,
        out_shape=jax.ShapeDtypeStruct((seq_len, width), jnp.bfloat16),
        in_specs=[
            pl.BlockSpec(memory_space=pltpu.VMEM),
            pl.BlockSpec(memory_space=pltpu.VMEM),
            pl.BlockSpec(memory_space=pl.ANY),
        ],
        out_specs=pl.BlockSpec(memory_space=pltpu.VMEM),
        scratch_shapes=[
            pltpu.VMEM((chunks, n_mp, ROWS, width), jnp.bfloat16),
            pltpu.VMEM((n_mp, width, width), jnp.bfloat16),
            pltpu.VMEM((ROWS, width), jnp.float32),
            pltpu.VMEM((ROWS, 128), jnp.float32),
            pltpu.VMEM((chunks, ROWS, width), jnp.bfloat16),
            pltpu.SemaphoreType.DMA((n_mp,)),
            pltpu.SemaphoreType.DMA((chunks, n_mp)),
            pltpu.SemaphoreType.DMA((chunks, 8)),
            pltpu.SemaphoreType.DMA((seq_len // ROWS,)),
            pltpu.SemaphoreType.DMA((seq_len // ROWS,)),
        ],
        compiler_params=pltpu.CompilerParams(
            collective_id=0, has_side_effects=True, vmem_limit_bytes=56 * 2**20
        ),
    )(stream, gain.reshape(n_mp, width), weight.reshape(n_mp, width, width))


def per_device(
    patches,
    ln_gain,
    ln_bias,
    w_merge_in,
    b_merge_in,
    w_merge_out,
    b_merge_out,
    text_rows,
    section_gain,
    section_weight,
    image_sizes,
    placement,
    offsets,
):
    n_section = lax.axis_size("section")
    n_dp = lax.axis_size("dp")
    n_mp = lax.axis_size("mp")
    section_pos = lax.axis_index("section")
    dp_pos = lax.axis_index("dp")
    mp_pos = lax.axis_index("mp")
    rows_enc = patches.shape[0]
    feat_width = w_merge_out.shape[1]
    own_width = feat_width // n_mp
    piece_width = own_width // n_section
    k_pair = K_PAIR
    slot_len = SLOT
    seq_len = n_dp * k_pair * slot_len
    owners_all = n_section * n_dp
    encoded = layer_norm(patches, ln_gain, ln_bias)
    hidden = jax.nn.gelu(
        jnp.dot(encoded, w_merge_in, preferred_element_type=jnp.float32) + b_merge_in,
        approximate=False,
    ).astype(jnp.bfloat16)
    partial_value = jnp.dot(hidden, w_merge_out, preferred_element_type=jnp.float32)
    my_sizes = lax.dynamic_slice_in_dim(image_sizes, dp_pos, 1, 0)
    my_place = lax.dynamic_slice_in_dim(placement, dp_pos, 1, 0)
    my_offsets = lax.dynamic_slice_in_dim(offsets, dp_pos, 1, 0)
    send_src, send_in = slot_layout(
        my_sizes,
        my_place,
        my_offsets,
        jnp.arange(owners_all, dtype=jnp.int32),
        k_pair,
        slot_len,
        rows_enc,
    )
    send_src = send_src.reshape(owners_all, k_pair * slot_len)
    send_in = send_in.reshape(owners_all, k_pair * slot_len)
    owner_here = jnp.reshape(section_pos * n_dp + dp_pos, (1,))
    recv_src, recv_in = slot_layout(
        image_sizes, placement, offsets, owner_here, k_pair, slot_len, rows_enc
    )
    recv_in = recv_in.reshape(seq_len)
    ordered = (
        partial_value.reshape(rows_enc, n_mp, n_section, piece_width)
        .transpose(0, 2, 1, 3)
        .reshape(rows_enc, feat_width)
    )
    summed = lax.psum_scatter(
        ordered.astype(jnp.bfloat16), ("section", "mp"), scatter_dimension=1, tiled=True
    ).astype(jnp.float32)
    bias_piece = lax.dynamic_slice_in_dim(
        b_merge_out, mp_pos * own_width + section_pos * piece_width, piece_width, 0
    )
    merged = (summed + bias_piece).astype(jnp.bfloat16)
    outgoing = jnp.where(send_in[..., None], merged[send_src], jnp.zeros((), jnp.bfloat16))
    arrived = lax.all_to_all(outgoing, ("section", "dp"), split_axis=0, concat_axis=0, tiled=True)
    image_part = (
        arrived.reshape(n_section, n_dp, k_pair * slot_len, piece_width)
        .transpose(1, 2, 0, 3)
        .reshape(seq_len, own_width)
    )
    stream = jnp.where(recv_in[:, None], image_part, text_rows.reshape(seq_len, own_width))
    result = layers(stream, section_gain, section_weight, n_section, n_mp)
    return result.reshape(1, 1, seq_len, own_width)


def solution(mesh):
    in_specs = (
        P("dp", None),
        P(),
        P(),
        P(None, ("section", "mp")),
        P(("section", "mp")),
        P(("section", "mp"), None),
        P(),
        P("section", "dp", None, "mp"),
        P("section", None),
        P("section", None, "mp"),
        P(),
        P(),
        P(),
    )
    out_specs = P("section", "dp", None, "mp")
    return jax.shard_map(
        per_device, mesh=mesh, in_specs=in_specs, out_specs=out_specs, check_vma=False
    )
```

```python
import jax
import jax.numpy as jnp
from jax import lax
from jax.experimental import pallas as pl
from jax.experimental.pallas import tpu as pltpu
from jax.sharding import PartitionSpec as P

SLOT = 8
K_PAIR = 4
ROWS = 64
PARTS = 2
MESH = pl.DeviceIdType.MESH
F32 = jnp.float32
BF16 = jnp.bfloat16


def place(slots, sizes, places, starts_at):
    count = sizes.shape[1]
    images = lax.broadcasted_iota(jnp.int32, (slots.shape[0], count), 1)
    match = places == slots // SLOT

    def picked(values):
        return jnp.sum(jnp.where(match, values, 0), axis=1, keepdims=True)

    image = picked(images)
    extent = picked(sizes)
    first = jnp.sum(jnp.where(images < image, sizes, 0), axis=1, keepdims=True)
    column = lax.rem(slots, SLOT) - jnp.minimum(picked(starts_at), SLOT - extent)
    return first + column, (column >= 0) & (column < extent)


def kernel(
    patches_hbm, ln_gain_ref, ln_bias_ref, w_in_hbm, b_in_ref, w_out_hbm, b_out_ref, text_ref,
    gain_ref, weight_hbm, sizes_ref, places_ref, offsets_ref,
    out_ref,
    patches, encoded, w_in, w_out, hidden, out1, in1, out2, in2, own, piece, picks, placed, images, text, texts,
    shards, weight, total, squares, results,
    load_sem, w_out_sem, hid_sem, rs1_sent, rs1_got, rs2_sent, rs2_got, text_sent, text_got, place_sent, image_got,
    weight_sem, got, sent, home_sem,
):
    section, dp, mp = (lax.axis_index(a) for a in ("section", "dp", "mp"))
    n_section, n_dp, n_mp = (lax.axis_size(a) for a in ("section", "dp", "mp"))
    n_ring = n_mp // 2
    chip, core = mp // 2, lax.rem(mp, 2)
    chunks, _, rows, width = shards.shape
    per_micro = chunks // n_section
    seq_len = rows * per_micro
    per_group = K_PAIR * SLOT
    rows_enc, inner = patches.shape
    features = ln_gain_ref.shape[1]
    half_rows = rows_enc // 2
    sub = width // n_section
    span = width // PARTS

    def at(chip_pos, core_pos):
        return lax.rem(chip_pos + n_ring, n_ring) * 2 + core_pos

    ahead, behind = at(chip + 1, core), at(chip - 1, core)
    sibling = at(chip, 1 - core)
    turn = 1 - 2 * core
    onward, source = at(chip + turn, core), at(chip - turn, core)
    far = at(chip + 2, core)

    def load(src, dst, slot):
        return pltpu.make_async_copy(src, dst, load_sem.at[slot])

    def load_weight(idx):
        return pltpu.make_async_copy(weight_hbm.at[idx], weight.at[idx], weight_sem.at[idx])

    barrier = pltpu.get_barrier_semaphore()

    def greet(**target):
        pl.semaphore_signal(barrier, inc=1, device_id=target, device_id_type=MESH)

    load(w_in_hbm, w_in, 0).start()
    load(patches_hbm, patches, 1).start()
    for partner in (ahead, behind, sibling):
        greet(mp=partner)

    @pl.when(section == 0)
    def _():
        for there in range(n_section):
            for hop in range(n_dp):
                if there or hop:
                    greet(section=there, dp=lax.rem(dp + hop, n_dp))

    @pl.when(section != 0)
    def _():
        for hop in range(n_dp):
            greet(section=0, dp=lax.rem(dp + hop, n_dp))
        for hop in range(1, n_section):
            there = lax.rem(section + hop, n_section)

            @pl.when(there != 0)
            def _():
                greet(section=there)

    def w_out_block(chip_pos, core_pos):
        columns = pl.multiple_of((chip_pos * 2 + core_pos) * width, width)
        return w_out_hbm.at[:, pl.ds(columns, width)]

    def w_out_own(chip_pos):
        return pltpu.make_async_copy(w_out_block(chip_pos, core), w_out.at[0, chip_pos], w_out_sem.at[0, chip_pos])

    def w_out_other(chip_pos):
        return pltpu.make_async_remote_copy(
            src_ref=w_out_block(chip_pos, 1 - core), dst_ref=w_out.at[1, chip_pos],
            send_sem=w_out_sem.at[1, chip_pos], recv_sem=w_out_sem.at[2, chip_pos],
            device_id={"mp": sibling}, device_id_type=MESH,
        )

    for chip_pos in range(n_ring):
        w_out_own(chip_pos).start()

    position = lax.broadcasted_iota(jnp.int32, (seq_len, 1), 0)
    group = position // per_group
    owner = section * n_dp + dp
    slots = owner * per_group + lax.rem(position, per_group)

    def by_group(ref):
        values = jnp.broadcast_to(ref[0:1, :], (seq_len, ref.shape[1]))
        for e in range(1, n_dp):
            values = jnp.where(group == e, ref[e : e + 1, :], values)
        return values

    _, covered = place(slots, by_group(sizes_ref), by_group(places_ref), by_group(offsets_ref))
    text[...] = jnp.where(covered, jnp.zeros((), F32), text_ref[...].astype(F32)).astype(BF16)

    everywhere = lax.broadcasted_iota(jnp.int32, (n_section * n_dp * per_group, 1), 0)
    mine = pl.ds(dp, 1)
    row, covered = place(everywhere, sizes_ref[mine, :], places_ref[mine, :], offsets_ref[mine, :])
    candidates = lax.broadcasted_iota(jnp.int32, (everywhere.shape[0], rows_enc), 1)
    picks[...] = jnp.where((candidates == row) & covered, 1.0, 0.0).astype(BF16)

    pl.semaphore_wait(barrier, jnp.where(section == 0, n_section * n_dp + 2, n_dp + n_section + 1))

    for chip_pos in range(n_ring):
        w_out_other(chip_pos).start()

    def feed():
        return pltpu.make_async_remote_copy(
            src_ref=text, dst_ref=texts.at[section],
            send_sem=text_sent, recv_sem=text_got.at[section],
            device_id={"section": 0}, device_id_type=MESH,
        )

    @pl.when(section != 0)
    def _():
        feed().start()

    @pl.when(section == 0)
    def _():
        pltpu.make_async_copy(text, texts.at[0], text_got.at[0]).start()

    for idx in range(n_mp):
        load_weight(idx).start()

    load(patches_hbm, patches, 1).wait()
    block = 16

    def norm(b, carry):
        here = pl.ds(pl.multiple_of(b * block, block), block)
        for q in range(inner // features):
            columns = slice(q * features, (q + 1) * features)
            values = patches[here, columns].astype(F32)
            centre = values - jnp.mean(values, axis=-1, keepdims=True)
            spread = jnp.mean(centre * centre, axis=-1, keepdims=True)
            normed = centre * lax.rsqrt(spread + 1e-06) * ln_gain_ref[...] + ln_bias_ref[...]
            encoded[here, columns] = normed.astype(BF16)
        return carry

    lax.fori_loop(0, rows_enc // block, norm, 0)
    load(w_in_hbm, w_in, 0).wait()
    before = lax.dot_general(
        encoded[...], w_in[...], (((1,), (1,)), ((), ())), preferred_element_type=F32
    ) + b_in_ref[...]
    hidden[0] = (0.5 * before * (1.0 + lax.erf(before * (0.5**0.5)))).astype(BF16)

    swap = pltpu.make_async_remote_copy(
        src_ref=hidden.at[0], dst_ref=hidden.at[1], send_sem=hid_sem.at[0], recv_sem=hid_sem.at[1],
        device_id={"mp": sibling}, device_id_type=MESH,
    )
    swap.start()
    for chip_pos in range(n_ring):
        w_out_own(chip_pos).wait()
    for chip_pos in range(n_ring):
        w_out_other(chip_pos).wait_recv()
    swap.wait_recv()

    def along(axis, delta):
        if axis:
            return {"section": lax.rem(section + delta + n_section, n_section)}
        return {"mp": at(chip + delta, core)}

    def spot(axis, delta):
        return lax.rem((section if axis else chip) + delta + n_ring, n_ring)

    def partial(h, idx, p):
        def product(k, chip_pos, columns):
            return jnp.dot(
                hidden[k, h * half_rows : (h + 1) * half_rows, :], w_out[k, chip_pos, :, columns],
                preferred_element_type=F32,
            )

        if h == 0:
            columns = slice(p * span, (p + 1) * span)
            return product(0, idx, columns) + product(1, idx, columns)
        columns = pl.ds(pl.multiple_of(idx * sub, sub), sub)
        count = span // sub
        return jnp.concatenate(
            [product(0, z, columns) + product(1, z, columns) for z in range(p * count, (p + 1) * count)], axis=1
        )

    def rs1(h, kind, p, delta):
        return pltpu.make_async_remote_copy(
            src_ref=out1.at[h, kind, p], dst_ref=in1.at[h, kind, p],
            send_sem=rs1_sent.at[h, kind, p], recv_sem=rs1_got.at[h, kind, p],
            device_id=along(h, delta), device_id_type=MESH,
        )

    def rs2(h, kind, delta):
        return pltpu.make_async_remote_copy(
            src_ref=out2.at[h, kind], dst_ref=in2.at[h, kind],
            send_sem=rs2_sent.at[h, kind], recv_sem=rs2_got.at[h, kind],
            device_id=along(1 - h, delta), device_id_type=MESH,
        )

    FAR, NEAR, SUM = 0, 1, 2
    for p in range(PARTS):
        for h in range(2):
            out1[h, FAR, p] = partial(h, spot(h, 2), p).astype(BF16)
            rs1(h, FAR, p, turn).start()
    for p in range(PARTS):
        for h in range(2):
            out1[h, NEAR, p] = partial(h, spot(h, -turn), p).astype(BF16)
            rs1(h, NEAR, p, -turn).start()
    for p in range(PARTS):
        for h in range(2):
            value = partial(h, spot(h, turn), p)
            rs1(h, FAR, p, turn).wait_recv()
            out1[h, SUM, p] = (value + in1[h, FAR, p].astype(F32)).astype(BF16)
            rs1(h, SUM, p, turn).start()
    for p in range(PARTS):
        for h in range(2):
            own[h, :, p * span : (p + 1) * span] = partial(h, spot(h, 0), p)
    for p in range(PARTS):
        for h in range(2):
            columns = slice(p * span, (p + 1) * span)
            rs1(h, NEAR, p, -turn).wait_recv()
            rs1(h, SUM, p, turn).wait_recv()
            own[h, :, columns] += in1[h, NEAR, p].astype(F32) + in1[h, SUM, p].astype(F32)

    def own_block(h, delta):
        columns = pl.ds(pl.multiple_of(spot(1 - h, delta) * sub, sub), sub)
        return own[h, :, columns]

    for h in range(2):
        out2[h, FAR] = own_block(h, 2).astype(BF16)
        rs2(h, FAR, turn).start()
        out2[h, NEAR] = own_block(h, -turn).astype(BF16)
        rs2(h, NEAR, -turn).start()
    for h in range(2):
        value = own_block(h, turn)
        rs2(h, FAR, turn).wait_recv()
        out2[h, SUM] = (value + in2[h, FAR].astype(F32)).astype(BF16)
        rs2(h, SUM, turn).start()
    bias = b_out_ref[pl.ds(mp * n_section + section, 1), :]
    for h in range(2):
        value = own_block(h, 0)
        rs2(h, NEAR, -turn).wait_recv()
        rs2(h, SUM, turn).wait_recv()
        value = value + in2[h, NEAR].astype(F32) + in2[h, SUM].astype(F32) + bias
        piece[h * half_rows : (h + 1) * half_rows, :] = value.astype(BF16)

    placed[...] = jnp.dot(picks[...], piece[...], preferred_element_type=F32).astype(BF16)

    def block_of(micro, seq):
        begin = pl.multiple_of((micro * n_dp + seq) * per_group, per_group)
        return placed.at[pl.ds(begin, per_group)]

    def landing(micro):
        return images.at[
            micro, pl.ds(pl.multiple_of(dp * per_group, per_group), per_group),
            pl.ds(pl.multiple_of(section * sub, sub), sub),
        ]

    part_of = dp * per_group // rows

    def deliver(micro, hop):
        seq = lax.rem(dp + hop, n_dp)
        return pltpu.make_async_remote_copy(
            src_ref=block_of(micro, seq), dst_ref=landing(micro),
            send_sem=place_sent.at[micro, hop], recv_sem=image_got.at[micro * per_micro + part_of],
            device_id={"section": 0, "dp": seq}, device_id_type=MESH,
        )

    for micro in range(n_section):
        for hop in range(n_dp):
            if hop:
                deliver(micro, hop).start()
            else:
                @pl.when(section != 0)
                def _():
                    deliver(micro, 0).start()

                @pl.when(section == 0)
                def _():
                    pltpu.make_async_copy(
                        block_of(micro, dp), landing(micro), image_got.at[micro * per_micro + part_of]
                    ).start()

    def shard_copy(t, idx, slot, **target):
        return pltpu.make_async_remote_copy(
            src_ref=shards.at[t, idx], dst_ref=shards.at[t, idx],
            send_sem=sent.at[t, slot], recv_sem=got.at[t, idx],
            device_id=target, device_id_type=MESH,
        )

    def arrival(t, idx):
        shard_copy(t, idx, 0, mp=sibling).wait_recv()

    def enter(t):
        micro, part = t // per_micro, lax.rem(t, per_micro)
        here = pl.ds(pl.multiple_of(part * rows, rows), rows)

        @pl.when(part == 0)
        def _():
            pltpu.make_async_remote_copy(
                src_ref=text, dst_ref=texts.at[micro], send_sem=text_sent, recv_sem=text_got.at[micro],
                device_id={"section": 0}, device_id_type=MESH,
            ).wait_recv()

        pltpu.make_async_remote_copy(
            src_ref=images.at[micro, here], dst_ref=images.at[micro, here],
            send_sem=text_sent, recv_sem=image_got.at[t],
            device_id={"section": 0}, device_id_type=MESH,
        ).wait_recv()
        shards[t, mp] = (images[micro, here, :].astype(F32) + texts[micro, here, :].astype(F32)).astype(BF16)

    def pass_on(t):
        return pltpu.make_async_remote_copy(
            src_ref=results.at[t], dst_ref=shards.at[t, mp],
            send_sem=sent.at[t, 7], recv_sem=got.at[t, mp],
            device_id={"section": section + 1}, device_id_type=MESH,
        )

    def bring_home(t):
        half = lax.rem(t, per_micro)
        return pltpu.make_async_remote_copy(
            src_ref=results.at[t], dst_ref=out_ref.at[pl.ds(pl.multiple_of(half * rows, rows), rows)],
            send_sem=sent.at[t, 7], recv_sem=home_sem.at[half],
            device_id={"section": t // per_micro}, device_id_type=MESH,
        )

    def add(t, idx):
        values = shards[t, idx].astype(F32)
        square = values * values
        lanes = squares[...]
        for j in range(0, width, 128):
            lanes = lanes + square[:, j : j + 128]
        squares[...] = lanes
        scaled = (values * gain_ref[pl.ds(idx, 1), :]).astype(BF16)
        total[...] += jnp.dot(scaled, weight[idx], preferred_element_type=F32)

    last = n_section - 1

    def turn_body(i, carry):
        t = i - 1

        @pl.when(i < chunks)
        def _():
            @pl.when(section == 0)
            def _():
                enter(i)

            @pl.when(section != 0)
            def _():
                arrival(i, mp)

            shard_copy(i, mp, 0, mp=onward).start()
            shard_copy(i, mp, 1, mp=source).start()
            shard_copy(i, mp, 2, mp=sibling).start()

        @pl.when(i == 1)
        def _():
            for idx in range(n_mp):
                load_weight(idx).wait()

        @pl.when(i > 0)
        def _():
            total[...] = jnp.zeros_like(total)
            squares[...] = jnp.zeros_like(squares)
            add(t, mp)
            add(t, source)
            add(t, onward)
            arrival(t, far)
            shard_copy(t, far, 3, mp=sibling).start()
            add(t, far)
            for step in (0, 1, -1):
                idx = at(chip + step, 1 - core)
                arrival(t, idx)
                add(t, idx)

        @pl.when(i < chunks)
        def _():
            arrival(i, source)
            shard_copy(i, source, 4, mp=onward).start()
            shard_copy(i, source, 5, mp=sibling).start()
            arrival(i, onward)
            shard_copy(i, onward, 6, mp=sibling).start()

        @pl.when(i > 0)
        def _():
            idx = at(chip + 2, 1 - core)
            arrival(t, idx)
            add(t, idx)
            square = jnp.sum(squares[...], axis=-1, keepdims=True) * (1.0 / (n_mp * width))
            update = total[...] * lax.rsqrt(square + 1e-06)
            result = (shards[t, mp].astype(F32) + update).astype(BF16)
            results[t] = result

            @pl.when(section < last)
            def _():
                pass_on(t).start()

            @pl.when((section == last) & (t < last * per_micro))
            def _():
                bring_home(t).start()

            @pl.when((section == last) & (t >= last * per_micro))
            def _():
                half = lax.rem(t, per_micro)
                out_ref[pl.ds(pl.multiple_of(half * rows, rows), rows)] = result

        return carry

    lax.fori_loop(0, chunks + 1, turn_body, 0)

    @pl.when(section < last)
    def _():
        for half in range(per_micro):
            bring_home(half).wait_recv()

    for chip_pos in range(n_ring):
        w_out_other(chip_pos).wait_send()
    swap.wait_send()
    for h in range(2):
        for kind in range(3):
            for p in range(PARTS):
                rs1(h, kind, p, 1).wait_send()
            rs2(h, kind, 1).wait_send()
    for micro in range(n_section):
        for hop in range(1, n_dp):
            deliver(micro, hop).wait_send()

    @pl.when(section != 0)
    def _():
        feed().wait_send()
        for micro in range(n_section):
            deliver(micro, 0).wait_send()

    def settle(t, carry):
        for slot in range(7):
            shard_copy(t, mp, slot, mp=sibling).wait_send()

        @pl.when((section < last) | (t < last * per_micro))
        def _():
            shard_copy(t, mp, 7, mp=sibling).wait_send()

        return carry

    lax.fori_loop(0, chunks, settle, 0)


def per_device(
    n_section,
    n_dp,
    n_mp,
    patches,
    ln_gain,
    ln_bias,
    w_merge_in,
    b_merge_in,
    w_merge_out,
    b_merge_out,
    text_rows,
    section_gain,
    section_weight,
    image_sizes,
    placement,
    offsets,
):
    rows_enc, inner = patches.shape
    depth, features_out = w_merge_out.shape
    seq_len, width = text_rows.shape[2:]
    n_ring = n_mp // 2
    sub = width // n_section
    half = rows_enc // 2
    chunks = n_section * seq_len // ROWS
    per_micro = seq_len // ROWS
    slots = n_section * n_dp * K_PAIR * SLOT
    dma = pltpu.SemaphoreType.DMA
    vmem = pl.BlockSpec(memory_space=pltpu.VMEM)
    hbm = pl.BlockSpec(memory_space=pl.ANY)
    out = pl.pallas_call(
        kernel,
        out_shape=jax.ShapeDtypeStruct((seq_len, width), BF16),
        in_specs=[hbm, vmem, vmem, hbm, vmem, hbm, vmem, vmem, vmem, hbm, vmem, vmem, vmem],
        out_specs=vmem,
        scratch_shapes=[
            pltpu.VMEM((rows_enc, inner), BF16),
            pltpu.VMEM((rows_enc, inner), BF16),
            pltpu.VMEM((depth, inner), BF16),
            pltpu.VMEM((2, n_ring, depth, width), BF16),
            pltpu.VMEM((2, rows_enc, depth), BF16),
            pltpu.VMEM((2, 3, PARTS, half, width // PARTS), BF16),
            pltpu.VMEM((2, 3, PARTS, half, width // PARTS), BF16),
            pltpu.VMEM((2, 3, half, sub), BF16),
            pltpu.VMEM((2, 3, half, sub), BF16),
            pltpu.VMEM((2, half, width), F32),
            pltpu.VMEM((rows_enc, sub), BF16),
            pltpu.VMEM((slots, rows_enc), BF16),
            pltpu.VMEM((slots, sub), BF16),
            pltpu.VMEM((n_section, seq_len, width), BF16),
            pltpu.VMEM((seq_len, width), BF16),
            pltpu.VMEM((n_section, seq_len, width), BF16),
            pltpu.VMEM((chunks, n_mp, ROWS, width), BF16),
            pltpu.VMEM((n_mp, width, width), BF16),
            pltpu.VMEM((ROWS, width), F32),
            pltpu.VMEM((ROWS, 128), F32),
            pltpu.VMEM((chunks, ROWS, width), BF16),
            dma((2,)),
            dma((3, n_ring)),
            dma((2,)),
            dma((2, 3, PARTS)),
            dma((2, 3, PARTS)),
            dma((2, 3)),
            dma((2, 3)),
            dma,
            dma((n_section,)),
            dma((n_section, n_dp)),
            dma((chunks,)),
            dma((n_mp,)),
            dma((chunks, n_mp)),
            dma((chunks, 8)),
            dma((per_micro,)),
        ],
        compiler_params=pltpu.CompilerParams(
            collective_id=0, has_side_effects=True, vmem_limit_bytes=60 * 2**20
        ),
    )(
        patches,
        ln_gain.reshape(1, -1),
        ln_bias.reshape(1, -1),
        w_merge_in.T,
        b_merge_in.reshape(1, -1),
        w_merge_out,
        b_merge_out.reshape(n_mp * n_section, sub),
        text_rows.reshape(seq_len, width),
        section_gain.reshape(n_mp, width),
        section_weight.reshape(n_mp, width, width),
        image_sizes,
        placement,
        offsets,
    )
    return out.reshape(1, 1, seq_len, width)


def solution(mesh):
    in_specs = (
        P("dp", None),
        P(),
        P(),
        P(None, ("section", "mp")),
        P(("section", "mp")),
        P(("section", "mp"), None),
        P(),
        P("section", "dp", None, "mp"),
        P("section", None),
        P("section", None, "mp"),
        P(),
        P(),
        P(),
    )
    out_specs = P("section", "dp", None, "mp")
    sizes = (mesh.shape["section"], mesh.shape["dp"], mesh.shape["mp"])

    def run(*arrays):
        return per_device(*sizes, *arrays)

    return jax.shard_map(run, mesh=mesh, in_specs=in_specs, out_specs=out_specs, check_vma=False)
```

```python
import jax
import jax.numpy as jnp
from jax import lax
from jax.experimental import pallas as pl
from jax.experimental.pallas import tpu as pltpu
from jax.sharding import PartitionSpec as P

SLOT = 8
K_PAIR = 4
ROWS = 32
TALL = 128
LAG = 2
PARTS = 2
MESH = pl.DeviceIdType.MESH
F32 = jnp.float32
BF16 = jnp.bfloat16


def place(slots, sizes, places, starts_at):
    count = sizes.shape[1]
    images = lax.broadcasted_iota(jnp.int32, (slots.shape[0], count), 1)
    match = places == slots // SLOT

    def picked(values):
        return jnp.sum(jnp.where(match, values, 0), axis=1, keepdims=True)

    image = picked(images)
    extent = picked(sizes)
    first = jnp.sum(jnp.where(images < image, sizes, 0), axis=1, keepdims=True)
    column = lax.rem(slots, SLOT) - jnp.minimum(picked(starts_at), SLOT - extent)
    return first + column, (column >= 0) & (column < extent)


def kernel(
    patches_hbm, ln_gain_ref, ln_bias_ref, w_in_hbm, b_in_ref, w_out_hbm, b_out_ref, text_ref,
    gain_ref, weight_hbm, sizes_ref, places_ref, offsets_ref,
    out_ref,
    patches, encoded, w_in, w_out, w_lent, hidden, out1, in1, out2, in2, own, piece, picks, placed, images, text, texts,
    shards, weight, tall, total, squares, results,
    load_sem, w_out_sem, hid_sem, rs1_sent, rs1_got, rs2_sent, rs2_got, text_sent, text_got, place_sent, image_got,
    weight_sem, got, sent, home_sem,
):
    section, dp, mp = (lax.axis_index(a) for a in ("section", "dp", "mp"))
    n_section, n_dp, n_mp = (lax.axis_size(a) for a in ("section", "dp", "mp"))
    n_ring = n_mp // 2
    chip, core = mp // 2, lax.rem(mp, 2)
    chunks, _, rows, width = shards.shape
    per_micro = chunks // n_section
    seq_len = rows * per_micro
    per_group = K_PAIR * SLOT
    rows_enc, inner = patches.shape
    features = ln_gain_ref.shape[0] * 128
    half_rows = rows_enc // 2
    sub = width // n_section
    span = width // PARTS

    def at(chip_pos, core_pos):
        return lax.rem(chip_pos + n_ring, n_ring) * 2 + core_pos

    ahead, behind = at(chip + 1, core), at(chip - 1, core)
    sibling = at(chip, 1 - core)
    turn = 1 - 2 * core
    onward, source = at(chip + turn, core), at(chip - turn, core)
    far = at(chip + 2, core)

    def load(src, dst, slot):
        return pltpu.make_async_copy(src, dst, load_sem.at[slot])

    def load_weight(idx):
        return pltpu.make_async_copy(weight_hbm.at[idx], weight.at[idx], weight_sem.at[idx])

    barrier = pltpu.get_barrier_semaphore()

    def greet(**target):
        pl.semaphore_signal(barrier, inc=1, device_id=target, device_id_type=MESH)

    load(w_in_hbm, w_in, 0).start()
    load(patches_hbm, patches, 1).start()
    for partner in (ahead, behind, sibling):
        greet(mp=partner)

    @pl.when(section == 0)
    def _():
        for there in range(n_section):
            for hop in range(n_dp):
                if there or hop:
                    greet(section=there, dp=lax.rem(dp + hop, n_dp))

    @pl.when(section != 0)
    def _():
        for hop in range(n_dp):
            greet(section=0, dp=lax.rem(dp + hop, n_dp))
        for hop in range(1, n_section):
            there = lax.rem(section + hop, n_section)

            @pl.when(there != 0)
            def _():
                greet(section=there)

    def w_out_block(chip_pos, core_pos):
        columns = pl.multiple_of((chip_pos * 2 + core_pos) * width, width)
        return w_out_hbm.at[:, pl.ds(columns, width)]

    def w_out_own(chip_pos):
        return pltpu.make_async_copy(w_out_block(chip_pos, core), w_out.at[0, chip_pos], w_out_sem.at[0, chip_pos])

    def w_out_fetch(chip_pos):
        return pltpu.make_async_copy(w_out_block(chip_pos, 1 - core), w_lent.at[chip_pos], w_out_sem.at[3, chip_pos])

    def w_out_other(chip_pos):
        return pltpu.make_async_remote_copy(
            src_ref=w_lent.at[chip_pos], dst_ref=w_out.at[1, chip_pos],
            send_sem=w_out_sem.at[1, chip_pos], recv_sem=w_out_sem.at[2, chip_pos],
            device_id={"mp": sibling}, device_id_type=MESH,
        )

    for chip_pos in range(n_ring):
        w_out_fetch(chip_pos).start()
    for chip_pos in range(n_ring):
        w_out_own(chip_pos).start()

    position = lax.broadcasted_iota(jnp.int32, (seq_len, 1), 0)
    group = position // per_group
    owner = section * n_dp + dp
    slots = owner * per_group + lax.rem(position, per_group)

    def by_group(ref):
        values = jnp.broadcast_to(ref[0:1, :], (seq_len, ref.shape[1]))
        for e in range(1, n_dp):
            values = jnp.where(group == e, ref[e : e + 1, :], values)
        return values

    _, covered = place(slots, by_group(sizes_ref), by_group(places_ref), by_group(offsets_ref))
    text[...] = jnp.where(covered, jnp.zeros((), F32), text_ref[...].astype(F32)).astype(BF16)

    everywhere = lax.broadcasted_iota(jnp.int32, (n_section * n_dp * per_group, 1), 0)
    mine = pl.ds(dp, 1)
    row, covered = place(everywhere, sizes_ref[mine, :], places_ref[mine, :], offsets_ref[mine, :])
    candidates = lax.broadcasted_iota(jnp.int32, (everywhere.shape[0], rows_enc), 1)
    picks[...] = jnp.where((candidates == row) & covered, 1.0, 0.0).astype(BF16)

    for idx in range(n_mp):
        load_weight(idx).start()

    def one_row(ref, begin, count):
        return jnp.concatenate([ref[pl.ds(begin + k, 1), :] for k in range(count)], axis=1)

    ln_gain = one_row(ln_gain_ref, 0, features // 128)
    ln_bias = one_row(ln_bias_ref, 0, features // 128)
    load(patches_hbm, patches, 1).wait()
    block = 16

    def norm(b, carry):
        here = pl.ds(pl.multiple_of(b * block, block), block)
        for q in range(inner // features):
            columns = slice(q * features, (q + 1) * features)
            values = patches[here, columns].astype(F32)
            centre = values - jnp.mean(values, axis=-1, keepdims=True)
            spread = jnp.mean(centre * centre, axis=-1, keepdims=True)
            normed = centre * lax.rsqrt(spread + 1e-06) * ln_gain + ln_bias
            encoded[here, columns] = normed.astype(BF16)
        return carry

    lax.fori_loop(0, rows_enc // block, norm, 0)
    pl.semaphore_wait(barrier, jnp.where(section == 0, n_section * n_dp + 2, n_dp + n_section + 1))

    for chip_pos in range(n_ring):
        w_out_fetch(chip_pos).wait()
        w_out_other(chip_pos).start()

    load(w_in_hbm, w_in, 0).wait()
    before = lax.dot_general(
        encoded[...], w_in[...], (((1,), (1,)), ((), ())), preferred_element_type=F32
    ) + b_in_ref[...]
    hidden[0] = (0.5 * before * (1.0 + lax.erf(before * (0.5**0.5)))).astype(BF16)

    swap = pltpu.make_async_remote_copy(
        src_ref=hidden.at[0], dst_ref=hidden.at[1], send_sem=hid_sem.at[0], recv_sem=hid_sem.at[1],
        device_id={"mp": sibling}, device_id_type=MESH,
    )
    swap.start()
    for chip_pos in range(n_ring):
        w_out_own(chip_pos).wait()
    for chip_pos in range(n_ring):
        w_out_other(chip_pos).wait_recv()
    swap.wait_recv()

    def along(axis, delta):
        if axis:
            return {"section": lax.rem(section + delta + n_section, n_section)}
        return {"mp": at(chip + delta, core)}

    def spot(axis, delta):
        return lax.rem((section if axis else chip) + delta + n_ring, n_ring)

    def partial(h, idx, p):
        def product(k, chip_pos, columns):
            return jnp.dot(
                hidden[k, h * half_rows : (h + 1) * half_rows, :], w_out[k, chip_pos, :, columns],
                preferred_element_type=F32,
            )

        if h == 0:
            columns = slice(p * span, (p + 1) * span)
            return product(0, idx, columns) + product(1, idx, columns)
        columns = pl.ds(pl.multiple_of(idx * sub, sub), sub)
        count = span // sub
        return jnp.concatenate(
            [product(0, z, columns) + product(1, z, columns) for z in range(p * count, (p + 1) * count)], axis=1
        )

    def rs1(h, kind, p, delta):
        return pltpu.make_async_remote_copy(
            src_ref=out1.at[h, kind, p], dst_ref=in1.at[h, kind, p],
            send_sem=rs1_sent.at[h, kind, p], recv_sem=rs1_got.at[h, kind, p],
            device_id=along(h, delta), device_id_type=MESH,
        )

    def rs2(h, kind, delta):
        return pltpu.make_async_remote_copy(
            src_ref=out2.at[h, kind], dst_ref=in2.at[h, kind],
            send_sem=rs2_sent.at[h, kind], recv_sem=rs2_got.at[h, kind],
            device_id=along(1 - h, delta), device_id_type=MESH,
        )

    FAR, NEAR, SUM = 0, 1, 2
    for p in range(PARTS):
        for h in range(2):
            out1[h, FAR, p] = partial(h, spot(h, 2), p).astype(BF16)
            rs1(h, FAR, p, turn).start()
    for p in range(PARTS):
        for h in range(2):
            out1[h, NEAR, p] = partial(h, spot(h, -turn), p).astype(BF16)
            rs1(h, NEAR, p, -turn).start()
    for p in range(PARTS):
        for h in range(2):
            value = partial(h, spot(h, turn), p)
            rs1(h, FAR, p, turn).wait_recv()
            out1[h, SUM, p] = (value + in1[h, FAR, p].astype(F32)).astype(BF16)
            rs1(h, SUM, p, turn).start()
    for p in range(PARTS):
        for h in range(2):
            own[h, :, p * span : (p + 1) * span] = partial(h, spot(h, 0), p)
    for p in range(PARTS):
        for h in range(2):
            columns = slice(p * span, (p + 1) * span)
            rs1(h, NEAR, p, -turn).wait_recv()
            rs1(h, SUM, p, turn).wait_recv()
            own[h, :, columns] += in1[h, NEAR, p].astype(F32) + in1[h, SUM, p].astype(F32)

    def own_block(h, delta):
        columns = pl.ds(pl.multiple_of(spot(1 - h, delta) * sub, sub), sub)
        return own[h, :, columns]

    for h in range(2):
        out2[h, FAR] = own_block(h, 2).astype(BF16)
        rs2(h, FAR, turn).start()
        out2[h, NEAR] = own_block(h, -turn).astype(BF16)
        rs2(h, NEAR, -turn).start()
    for h in range(2):
        value = own_block(h, turn)
        rs2(h, FAR, turn).wait_recv()
        out2[h, SUM] = (value + in2[h, FAR].astype(F32)).astype(BF16)
        rs2(h, SUM, turn).start()
    bias = one_row(b_out_ref, (mp * n_section + section) * (sub // 128), sub // 128)
    for h in range(2):
        value = own_block(h, 0)
        rs2(h, NEAR, -turn).wait_recv()
        rs2(h, SUM, turn).wait_recv()
        value = value + in2[h, NEAR].astype(F32) + in2[h, SUM].astype(F32) + bias
        piece[h * half_rows : (h + 1) * half_rows, :] = value.astype(BF16)

    placed[...] = jnp.dot(picks[...], piece[...], preferred_element_type=F32).astype(BF16)

    def block_of(micro, seq):
        begin = pl.multiple_of((micro * n_dp + seq) * per_group, per_group)
        return placed.at[pl.ds(begin, per_group)]

    def landing(micro):
        return images.at[
            micro, pl.ds(pl.multiple_of(dp * per_group, per_group), per_group),
            pl.ds(pl.multiple_of(section * sub, sub), sub),
        ]

    part_of = dp * per_group // rows

    def deliver(micro, hop):
        seq = lax.rem(dp + hop, n_dp)
        return pltpu.make_async_remote_copy(
            src_ref=block_of(micro, seq), dst_ref=landing(micro),
            send_sem=place_sent.at[micro, hop], recv_sem=image_got.at[micro * per_micro + part_of],
            device_id={"section": 0, "dp": seq}, device_id_type=MESH,
        )

    def feed():
        return pltpu.make_async_remote_copy(
            src_ref=text, dst_ref=texts.at[section],
            send_sem=text_sent, recv_sem=text_got.at[section],
            device_id={"section": 0}, device_id_type=MESH,
        )

    def keep(micro):
        pltpu.make_async_copy(
            block_of(micro, dp), landing(micro), image_got.at[micro * per_micro + part_of]
        ).start()

    def deliver_all(micro):
        for hop in range(n_dp):
            deliver(micro, hop).start()

    def delivered(micro):
        for hop in range(n_dp):
            deliver(micro, hop).wait_send()

    paced = 2

    @pl.when(section == 0)
    def _():
        pltpu.make_async_copy(text, texts.at[0], text_got.at[0]).start()
        keep(0)
        for hop in range(1, n_dp):
            deliver(0, hop).start()

    @pl.when(section != 0)
    def _():
        for micro in range(n_section):
            if micro:
                @pl.when(section == micro)
                def _():
                    feed().start()

            deliver_all(micro)
            if micro < paced:
                delivered(micro)

    def shard_copy(t, idx, slot, **target):
        return pltpu.make_async_remote_copy(
            src_ref=shards.at[t, idx], dst_ref=shards.at[t, idx],
            send_sem=sent.at[t, slot], recv_sem=got.at[t, idx],
            device_id=target, device_id_type=MESH,
        )

    def arrival(t, idx):
        shard_copy(t, idx, 0, mp=sibling).wait_recv()

    def enter(t):
        micro, part = t // per_micro, lax.rem(t, per_micro)
        here = pl.ds(pl.multiple_of(part * rows, rows), rows)

        @pl.when(part == 0)
        def _():
            pltpu.make_async_remote_copy(
                src_ref=text, dst_ref=texts.at[micro], send_sem=text_sent, recv_sem=text_got.at[micro],
                device_id={"section": 0}, device_id_type=MESH,
            ).wait_recv()

        pltpu.make_async_remote_copy(
            src_ref=images.at[micro, here], dst_ref=images.at[micro, here],
            send_sem=text_sent, recv_sem=image_got.at[t],
            device_id={"section": 0}, device_id_type=MESH,
        ).wait_recv()
        shards[t, mp] = (images[micro, here, :].astype(F32) + texts[micro, here, :].astype(F32)).astype(BF16)

    def pass_on(t):
        return pltpu.make_async_remote_copy(
            src_ref=results.at[t], dst_ref=shards.at[t, mp],
            send_sem=sent.at[t, 7], recv_sem=got.at[t, mp],
            device_id={"section": section + 1}, device_id_type=MESH,
        )

    def bring_home(t):
        half = lax.rem(t, per_micro)
        return pltpu.make_async_remote_copy(
            src_ref=results.at[t], dst_ref=out_ref.at[pl.ds(pl.multiple_of(half * rows, rows), rows)],
            send_sem=sent.at[t, 7], recv_sem=home_sem.at[half],
            device_id={"section": t // per_micro}, device_id_type=MESH,
        )

    def add(t, idx, first=False):
        values = shards[t, idx].astype(F32)
        square = values * values
        lanes = square[:, :128] if first else squares[...] + square[:, :128]
        for j in range(128, width, 128):
            lanes = lanes + square[:, j : j + 128]
        squares[...] = lanes
        gain = gain_ref[:, pl.ds(pl.multiple_of(idx * width, width), width)]
        tall[idx, 0:rows] = (values * gain).astype(BF16)
        update = jnp.dot(tall[idx], weight[idx], preferred_element_type=F32)[0:rows]
        total[...] = update if first else total[...] + update

    last = n_section - 1
    tall[...] = jnp.zeros_like(tall)

    def begin(t):
        @pl.when(section == 0)
        def _():
            enter(t)

        @pl.when(section != 0)
        def _():
            arrival(t, mp)

        shard_copy(t, mp, 0, mp=onward).start()
        shard_copy(t, mp, 1, mp=source).start()
        shard_copy(t, mp, 3, mp=far).start()
        shard_copy(t, mp, 2, mp=sibling).start()

    def share(t):
        for slot, idx in ((4, source), (5, onward), (6, far)):
            arrival(t, idx)
            shard_copy(t, idx, slot, mp=sibling).start()

    def multiply(t):
        add(t, mp, True)
        add(t, source)
        add(t, onward)
        add(t, far)
        for step in (0, -1, 1, 2):
            idx = at(chip + step * turn, 1 - core)
            arrival(t, idx)
            add(t, idx)
        square = jnp.sum(squares[...], axis=-1, keepdims=True) * (1.0 / (n_mp * width))
        update = total[...] * lax.rsqrt(square + 1e-06)
        result = (shards[t, mp].astype(F32) + update).astype(BF16)
        results[t] = result

        @pl.when(section < last)
        def _():
            pass_on(t).start()

        @pl.when((section == last) & (t < last * per_micro))
        def _():
            bring_home(t).start()

        @pl.when((section == last) & (t >= last * per_micro))
        def _():
            part = lax.rem(t, per_micro)
            out_ref[pl.ds(pl.multiple_of(part * rows, rows), rows)] = result

    def turn_body(i, carry):
        @pl.when(i < chunks)
        def _():
            begin(i)

        @pl.when((i == 1) & (section == 0))
        def _():
            for micro in range(1, n_section):
                keep(micro)
                for hop in range(1, n_dp):
                    deliver(micro, hop).start()

        @pl.when(i == LAG)
        def _():
            for idx in range(n_mp):
                load_weight(idx).wait()

        t = i - LAG

        @pl.when(t >= 0)
        def _():
            share(t)
            multiply(t)

        return carry

    lax.fori_loop(0, chunks + LAG, turn_body, 0)

    @pl.when(section < last)
    def _():
        for half in range(per_micro):
            bring_home(half).wait_recv()

    for chip_pos in range(n_ring):
        w_out_other(chip_pos).wait_send()
    swap.wait_send()
    for h in range(2):
        for kind in range(3):
            for p in range(PARTS):
                rs1(h, kind, p, 1).wait_send()
            rs2(h, kind, 1).wait_send()

    @pl.when(section == 0)
    def _():
        for micro in range(n_section):
            for hop in range(1, n_dp):
                deliver(micro, hop).wait_send()

    @pl.when(section != 0)
    def _():
        feed().wait_send()
        for micro in range(paced, n_section):
            delivered(micro)

    def settle(t, carry):
        for slot in range(7):
            shard_copy(t, mp, slot, mp=sibling).wait_send()

        @pl.when((section < last) | (t < last * per_micro))
        def _():
            shard_copy(t, mp, 7, mp=sibling).wait_send()

        return carry

    lax.fori_loop(0, chunks, settle, 0)


def per_device(
    n_section,
    n_dp,
    n_mp,
    patches,
    ln_gain,
    ln_bias,
    w_merge_in,
    b_merge_in,
    w_merge_out,
    b_merge_out,
    text_rows,
    section_gain,
    section_weight,
    image_sizes,
    placement,
    offsets,
):
    rows_enc, inner = patches.shape
    depth, features_out = w_merge_out.shape
    seq_len, width = text_rows.shape[2:]
    n_ring = n_mp // 2
    sub = width // n_section
    half = rows_enc // 2
    chunks = n_section * seq_len // ROWS
    per_micro = seq_len // ROWS
    slots = n_section * n_dp * K_PAIR * SLOT
    dma = pltpu.SemaphoreType.DMA
    vmem = pl.BlockSpec(memory_space=pltpu.VMEM)
    hbm = pl.BlockSpec(memory_space=pl.ANY)
    out = pl.pallas_call(
        kernel,
        out_shape=jax.ShapeDtypeStruct((seq_len, width), BF16),
        in_specs=[hbm, vmem, vmem, hbm, vmem, hbm, vmem, vmem, vmem, hbm, vmem, vmem, vmem],
        out_specs=vmem,
        scratch_shapes=[
            pltpu.VMEM((rows_enc, inner), BF16),
            pltpu.VMEM((rows_enc, inner), BF16),
            pltpu.VMEM((depth, inner), BF16),
            pltpu.VMEM((2, n_ring, depth, width), BF16),
            pltpu.VMEM((n_ring, depth, width), BF16),
            pltpu.VMEM((2, rows_enc, depth), BF16),
            pltpu.VMEM((2, 3, PARTS, half, width // PARTS), BF16),
            pltpu.VMEM((2, 3, PARTS, half, width // PARTS), BF16),
            pltpu.VMEM((2, 3, half, sub), BF16),
            pltpu.VMEM((2, 3, half, sub), BF16),
            pltpu.VMEM((2, half, width), F32),
            pltpu.VMEM((rows_enc, sub), BF16),
            pltpu.VMEM((slots, rows_enc), BF16),
            pltpu.VMEM((slots, sub), BF16),
            pltpu.VMEM((n_section, seq_len, width), BF16),
            pltpu.VMEM((seq_len, width), BF16),
            pltpu.VMEM((n_section, seq_len, width), BF16),
            pltpu.VMEM((chunks, n_mp, ROWS, width), BF16),
            pltpu.VMEM((n_mp, width, width), BF16),
            pltpu.VMEM((n_mp, TALL, width), BF16),
            pltpu.VMEM((ROWS, width), F32),
            pltpu.VMEM((ROWS, 128), F32),
            pltpu.VMEM((chunks, ROWS, width), BF16),
            dma((2,)),
            dma((4, n_ring)),
            dma((2,)),
            dma((2, 3, PARTS)),
            dma((2, 3, PARTS)),
            dma((2, 3)),
            dma((2, 3)),
            dma,
            dma((n_section,)),
            dma((n_section, n_dp)),
            dma((chunks,)),
            dma((n_mp,)),
            dma((chunks, n_mp)),
            dma((chunks, 8)),
            dma((per_micro,)),
        ],
        compiler_params=pltpu.CompilerParams(
            collective_id=0, has_side_effects=True, vmem_limit_bytes=60 * 2**20
        ),
    )(
        patches,
        ln_gain.reshape(-1, 128),
        ln_bias.reshape(-1, 128),
        w_merge_in.T,
        b_merge_in.reshape(1, -1),
        w_merge_out,
        b_merge_out.reshape(-1, 128),
        text_rows.reshape(seq_len, width),
        section_gain,
        section_weight.reshape(n_mp, width, width),
        image_sizes,
        placement,
        offsets,
    )
    return out.reshape(1, 1, seq_len, width)


def solution(mesh):
    in_specs = (
        P("dp", None),
        P(),
        P(),
        P(None, ("section", "mp")),
        P(("section", "mp")),
        P(("section", "mp"), None),
        P(),
        P("section", "dp", None, "mp"),
        P("section", None),
        P("section", None, "mp"),
        P(),
        P(),
        P(),
    )
    out_specs = P("section", "dp", None, "mp")
    sizes = (mesh.shape["section"], mesh.shape["dp"], mesh.shape["mp"])

    def run(*arrays):
        return per_device(*sizes, *arrays)

    return jax.shard_map(run, mesh=mesh, in_specs=in_specs, out_specs=out_specs, check_vma=False)
```

```python
import jax
import jax.numpy as jnp
from jax import lax
from jax.experimental import pallas as pl
from jax.experimental.pallas import tpu as pltpu
from jax.sharding import PartitionSpec as P

SLOT = 8
K_PAIR = 4
ROWS = 32
TALL = 128
LAG = 2
PARTS = 2
MESH = pl.DeviceIdType.MESH
F32 = jnp.float32
BF16 = jnp.bfloat16


def place(slots, sizes, places, starts_at):
    count = sizes.shape[1]
    images = lax.broadcasted_iota(jnp.int32, (slots.shape[0], count), 1)
    match = places == slots // SLOT

    def picked(values):
        return jnp.sum(jnp.where(match, values, 0), axis=1, keepdims=True)

    image = picked(images)
    extent = picked(sizes)
    first = jnp.sum(jnp.where(images < image, sizes, 0), axis=1, keepdims=True)
    column = lax.rem(slots, SLOT) - jnp.minimum(picked(starts_at), SLOT - extent)
    return first + column, (column >= 0) & (column < extent)


def kernel(
    patches_hbm, ln_gain_ref, ln_bias_ref, w_in_hbm, b_in_ref, w_out_hbm, b_out_ref, text_ref,
    gain_ref, weight_hbm, sizes_ref, places_ref, offsets_ref,
    out_ref,
    patches, encoded, w_in, w_out, w_lent, hidden, out1, in1, out2, in2, own, piece, picks, placed, images, text, texts,
    shards, weight, tall, total, squares, results,
    load_sem, w_out_sem, hid_sem, rs1_sent, rs1_got, rs2_sent, rs2_got, text_sent, text_got, place_sent, image_got,
    weight_sem, got, sent, home_sem,
):
    section, dp, mp = (lax.axis_index(a) for a in ("section", "dp", "mp"))
    n_section, n_dp, n_mp = (lax.axis_size(a) for a in ("section", "dp", "mp"))
    n_ring = n_mp // 2
    chip, core = mp // 2, lax.rem(mp, 2)
    chunks, _, _, rows, width = shards.shape
    per_micro = chunks // n_section
    seq_len = rows * per_micro
    per_group = K_PAIR * SLOT
    rows_enc, inner = patches.shape
    features = ln_gain_ref.shape[0] * 128
    half_rows = rows_enc // 2
    sub = width // n_section
    span = width // PARTS

    def at(chip_pos, core_pos):
        return lax.rem(chip_pos + n_ring, n_ring) * 2 + core_pos

    ahead, behind = at(chip + 1, core), at(chip - 1, core)
    sibling = at(chip, 1 - core)
    turn = 1 - 2 * core

    def load(src, dst, slot):
        return pltpu.make_async_copy(src, dst, load_sem.at[slot])

    def load_weight(idx):
        return pltpu.make_async_copy(weight_hbm.at[idx], weight.at[idx], weight_sem.at[idx])

    barrier = pltpu.get_barrier_semaphore()

    def greet(**target):
        pl.semaphore_signal(barrier, inc=1, device_id=target, device_id_type=MESH)

    load(w_in_hbm, w_in, 0).start()
    load(patches_hbm, patches, 1).start()
    for partner in (ahead, behind, sibling):
        greet(mp=partner)

    @pl.when(section == 0)
    def _():
        for there in range(n_section):
            for hop in range(n_dp):
                if there or hop:
                    greet(section=there, dp=lax.rem(dp + hop, n_dp))

    @pl.when(section != 0)
    def _():
        for hop in range(n_dp):
            greet(section=0, dp=lax.rem(dp + hop, n_dp))
        for hop in range(1, n_section):
            there = lax.rem(section + hop, n_section)

            @pl.when(there != 0)
            def _():
                greet(section=there)

    def w_out_block(chip_pos, core_pos):
        columns = pl.multiple_of((chip_pos * 2 + core_pos) * width, width)
        return w_out_hbm.at[:, pl.ds(columns, width)]

    def w_out_own(chip_pos):
        return pltpu.make_async_copy(w_out_block(chip_pos, core), w_out.at[0, chip_pos], w_out_sem.at[0, chip_pos])

    def w_out_fetch(chip_pos):
        return pltpu.make_async_copy(w_out_block(chip_pos, 1 - core), w_lent.at[chip_pos], w_out_sem.at[3, chip_pos])

    def w_out_other(chip_pos):
        return pltpu.make_async_remote_copy(
            src_ref=w_lent.at[chip_pos], dst_ref=w_out.at[1, chip_pos],
            send_sem=w_out_sem.at[1, chip_pos], recv_sem=w_out_sem.at[2, chip_pos],
            device_id={"mp": sibling}, device_id_type=MESH,
        )

    for chip_pos in range(n_ring):
        w_out_fetch(chip_pos).start()
    for chip_pos in range(n_ring):
        w_out_own(chip_pos).start()

    position = lax.broadcasted_iota(jnp.int32, (seq_len, 1), 0)
    group = position // per_group
    owner = section * n_dp + dp
    slots = owner * per_group + lax.rem(position, per_group)

    def by_group(ref):
        values = jnp.broadcast_to(ref[0:1, :], (seq_len, ref.shape[1]))
        for e in range(1, n_dp):
            values = jnp.where(group == e, ref[e : e + 1, :], values)
        return values

    _, covered = place(slots, by_group(sizes_ref), by_group(places_ref), by_group(offsets_ref))
    text[...] = jnp.where(covered, jnp.zeros((), F32), text_ref[...].astype(F32)).astype(BF16)

    everywhere = lax.broadcasted_iota(jnp.int32, (n_section * n_dp * per_group, 1), 0)
    mine = pl.ds(dp, 1)
    row, covered = place(everywhere, sizes_ref[mine, :], places_ref[mine, :], offsets_ref[mine, :])
    candidates = lax.broadcasted_iota(jnp.int32, (everywhere.shape[0], rows_enc), 1)
    picks[...] = jnp.where((candidates == row) & covered, 1.0, 0.0).astype(BF16)

    for idx in range(n_mp):
        load_weight(idx).start()

    def one_row(ref, begin, count):
        return jnp.concatenate([ref[pl.ds(begin + k, 1), :] for k in range(count)], axis=1)

    ln_gain = one_row(ln_gain_ref, 0, features // 128)
    ln_bias = one_row(ln_bias_ref, 0, features // 128)
    load(patches_hbm, patches, 1).wait()
    block = 16

    def norm(b, carry):
        here = pl.ds(pl.multiple_of(b * block, block), block)
        for q in range(inner // features):
            columns = slice(q * features, (q + 1) * features)
            values = patches[here, columns].astype(F32)
            centre = values - jnp.mean(values, axis=-1, keepdims=True)
            spread = jnp.mean(centre * centre, axis=-1, keepdims=True)
            normed = centre * lax.rsqrt(spread + 1e-06) * ln_gain + ln_bias
            encoded[here, columns] = normed.astype(BF16)
        return carry

    lax.fori_loop(0, rows_enc // block, norm, 0)
    pl.semaphore_wait(barrier, jnp.where(section == 0, n_section * n_dp + 2, n_dp + n_section + 1))

    for chip_pos in range(n_ring):
        w_out_fetch(chip_pos).wait()
        w_out_other(chip_pos).start()

    load(w_in_hbm, w_in, 0).wait()
    before = lax.dot_general(
        encoded[...], w_in[...], (((1,), (1,)), ((), ())), preferred_element_type=F32
    ) + b_in_ref[...]
    hidden[0] = (0.5 * before * (1.0 + lax.erf(before * (0.5**0.5)))).astype(BF16)

    swap = pltpu.make_async_remote_copy(
        src_ref=hidden.at[0], dst_ref=hidden.at[1], send_sem=hid_sem.at[0], recv_sem=hid_sem.at[1],
        device_id={"mp": sibling}, device_id_type=MESH,
    )
    swap.start()
    for chip_pos in range(n_ring):
        w_out_own(chip_pos).wait()
    for chip_pos in range(n_ring):
        w_out_other(chip_pos).wait_recv()
    swap.wait_recv()

    def along(axis, delta):
        if axis:
            return {"section": lax.rem(section + delta + n_section, n_section)}
        return {"mp": at(chip + delta, core)}

    def spot(axis, delta):
        return lax.rem((section if axis else chip) + delta + n_ring, n_ring)

    def partial(h, idx, p):
        def product(k, chip_pos, columns):
            return jnp.dot(
                hidden[k, h * half_rows : (h + 1) * half_rows, :], w_out[k, chip_pos, :, columns],
                preferred_element_type=F32,
            )

        if h == 0:
            columns = slice(p * span, (p + 1) * span)
            return product(0, idx, columns) + product(1, idx, columns)
        columns = pl.ds(pl.multiple_of(idx * sub, sub), sub)
        count = span // sub
        return jnp.concatenate(
            [product(0, z, columns) + product(1, z, columns) for z in range(p * count, (p + 1) * count)], axis=1
        )

    def rs1(h, kind, p, delta):
        return pltpu.make_async_remote_copy(
            src_ref=out1.at[h, kind, p], dst_ref=in1.at[h, kind, p],
            send_sem=rs1_sent.at[h, kind, p], recv_sem=rs1_got.at[h, kind, p],
            device_id=along(h, delta), device_id_type=MESH,
        )

    def rs2(h, kind):
        return pltpu.make_async_remote_copy(
            src_ref=out2.at[h, kind], dst_ref=in2.at[h, kind],
            send_sem=rs2_sent.at[h, kind], recv_sem=rs2_got.at[h, kind],
            device_id=along(1 - h, kind + 1), device_id_type=MESH,
        )

    FAR, NEAR, SUM = 0, 1, 2
    for p in range(PARTS):
        for h in range(2):
            out1[h, FAR, p] = partial(h, spot(h, 2), p).astype(BF16)
            rs1(h, FAR, p, turn).start()
    for p in range(PARTS):
        for h in range(2):
            out1[h, NEAR, p] = partial(h, spot(h, -turn), p).astype(BF16)
            rs1(h, FAR, p, turn).wait_send()
            rs1(h, NEAR, p, -turn).start()
    for p in range(PARTS):
        for h in range(2):
            value = partial(h, spot(h, turn), p)
            rs1(h, FAR, p, turn).wait_recv()
            out1[h, SUM, p] = (value + in1[h, FAR, p].astype(F32)).astype(BF16)
            rs1(h, SUM, p, turn).start()
    for p in range(PARTS):
        for h in range(2):
            own[h, :, p * span : (p + 1) * span] = partial(h, spot(h, 0), p)
    for p in range(PARTS):
        for h in range(2):
            columns = slice(p * span, (p + 1) * span)
            rs1(h, NEAR, p, -turn).wait_recv()
            rs1(h, SUM, p, turn).wait_recv()
            own[h, :, columns] += in1[h, NEAR, p].astype(F32) + in1[h, SUM, p].astype(F32)

    def own_block(h, delta):
        columns = pl.ds(pl.multiple_of(spot(1 - h, delta) * sub, sub), sub)
        return own[h, :, columns]

    for kind in (1, 0, 2):
        for h in range(2):
            out2[h, kind] = own_block(h, kind + 1).astype(BF16)
            rs2(h, kind).start()
    bias = one_row(b_out_ref, (mp * n_section + section) * (sub // 128), sub // 128)
    for h in range(2):
        value = own_block(h, 0) + bias
        for kind in (0, 2, 1):
            rs2(h, kind).wait_recv()
            value = value + in2[h, kind].astype(F32)
        piece[h * half_rows : (h + 1) * half_rows, :] = value.astype(BF16)

    placed[...] = jnp.dot(picks[...], piece[...], preferred_element_type=F32).astype(BF16)

    def block_of(micro, seq):
        begin = pl.multiple_of((micro * n_dp + seq) * per_group, per_group)
        return placed.at[pl.ds(begin, per_group)]

    def landing(micro):
        return images.at[
            micro, pl.ds(pl.multiple_of(dp * per_group, per_group), per_group),
            pl.ds(pl.multiple_of(section * sub, sub), sub),
        ]

    part_of = dp * per_group // rows

    def deliver(micro, hop):
        seq = lax.rem(dp + hop, n_dp)
        return pltpu.make_async_remote_copy(
            src_ref=block_of(micro, seq), dst_ref=landing(micro),
            send_sem=place_sent.at[micro, hop], recv_sem=image_got.at[micro * per_micro + part_of],
            device_id={"section": 0, "dp": seq}, device_id_type=MESH,
        )

    def feed():
        return pltpu.make_async_remote_copy(
            src_ref=text, dst_ref=texts.at[section],
            send_sem=text_sent, recv_sem=text_got.at[section],
            device_id={"section": 0}, device_id_type=MESH,
        )

    def keep(micro):
        pltpu.make_async_copy(
            block_of(micro, dp), landing(micro), image_got.at[micro * per_micro + part_of]
        ).start()

    def deliver_all(micro):
        for hop in range(n_dp):
            deliver(micro, hop).start()

    def delivered(micro):
        for hop in range(n_dp):
            deliver(micro, hop).wait_send()

    paced = 2

    @pl.when(section == 0)
    def _():
        pltpu.make_async_copy(text, texts.at[0], text_got.at[0]).start()
        keep(0)
        for hop in range(1, n_dp):
            deliver(0, hop).start()

    @pl.when(section != 0)
    def _():
        for micro in range(n_section):
            if micro:
                @pl.when(section == micro)
                def _():
                    feed().start()

            deliver_all(micro)
            if micro < paced:
                delivered(micro)

    def ring(step):
        return lax.rem(chip + step * turn + n_ring, n_ring)

    def shard_copy(t, step, slot):
        return pltpu.make_async_remote_copy(
            src_ref=shards.at[t, core, chip], dst_ref=shards.at[t, core, chip],
            send_sem=sent.at[t, slot], recv_sem=got.at[t, slot],
            device_id={"mp": at(chip + step * turn, core)}, device_id_type=MESH,
        )

    def entry(t):
        return pltpu.make_async_remote_copy(
            src_ref=results.at[t], dst_ref=shards.at[t, core, chip],
            send_sem=sent.at[t, 4], recv_sem=got.at[t, 4],
            device_id={"section": lax.rem(section + 1, n_section)}, device_id_type=MESH,
        )

    def lend(t):
        return pltpu.make_async_remote_copy(
            src_ref=shards.at[t, core], dst_ref=shards.at[t, core],
            send_sem=sent.at[t, 3], recv_sem=got.at[t, 3],
            device_id={"mp": sibling}, device_id_type=MESH,
        )

    def enter(t):
        micro, part = t // per_micro, lax.rem(t, per_micro)
        here = pl.ds(pl.multiple_of(part * rows, rows), rows)

        @pl.when(part == 0)
        def _():
            pltpu.make_async_remote_copy(
                src_ref=text, dst_ref=texts.at[micro], send_sem=text_sent, recv_sem=text_got.at[micro],
                device_id={"section": 0}, device_id_type=MESH,
            ).wait_recv()

        pltpu.make_async_remote_copy(
            src_ref=images.at[micro, here], dst_ref=images.at[micro, here],
            send_sem=text_sent, recv_sem=image_got.at[t],
            device_id={"section": 0}, device_id_type=MESH,
        ).wait_recv()
        shards[t, core, chip] = (images[micro, here, :].astype(F32) + texts[micro, here, :].astype(F32)).astype(BF16)

    def bring_home(t):
        half = lax.rem(t, per_micro)
        return pltpu.make_async_remote_copy(
            src_ref=results.at[t], dst_ref=out_ref.at[pl.ds(pl.multiple_of(half * rows, rows), rows)],
            send_sem=sent.at[t, 4], recv_sem=home_sem.at[half],
            device_id={"section": t // per_micro}, device_id_type=MESH,
        )

    def add(t, core_pos, chip_pos, first=False):
        idx = chip_pos * 2 + core_pos
        values = shards[t, core_pos, chip_pos].astype(F32)
        square = values * values
        lanes = square[:, :128] if first else squares[...] + square[:, :128]
        for j in range(128, width, 128):
            lanes = lanes + square[:, j : j + 128]
        squares[...] = lanes
        gain = gain_ref[:, pl.ds(pl.multiple_of(idx * width, width), width)]
        tall[idx, 0:rows] = (values * gain).astype(BF16)
        update = jnp.dot(tall[idx], weight[idx], preferred_element_type=F32)[0:rows]
        total[...] = update if first else total[...] + update

    last = n_section - 1
    tall[...] = jnp.zeros_like(tall)

    def begin(t):
        @pl.when(section == 0)
        def _():
            enter(t)

        @pl.when(section != 0)
        def _():
            entry(t).wait_recv()

        shard_copy(t, 1, 0).start()
        shard_copy(t, -1, 1).start()
        shard_copy(t, 2, 2).start()

    def share(t):
        for slot in range(3):
            shard_copy(t, 1, slot).wait_recv()
        lend(t).start()

    def multiply(t):
        for step in range(n_ring):
            add(t, core, ring(step), step == 0)
        lend(t).wait_recv()
        for step in range(n_ring):
            add(t, 1 - core, ring(step))
        square = jnp.sum(squares[...], axis=-1, keepdims=True) * (1.0 / (n_mp * width))
        update = total[...] * lax.rsqrt(square + 1e-06)
        result = (shards[t, core, chip].astype(F32) + update).astype(BF16)
        results[t] = result

        @pl.when(section < last)
        def _():
            entry(t).start()

        @pl.when((section == last) & (t < last * per_micro))
        def _():
            bring_home(t).start()

        @pl.when((section == last) & (t >= last * per_micro))
        def _():
            part = lax.rem(t, per_micro)
            out_ref[pl.ds(pl.multiple_of(part * rows, rows), rows)] = result

    def turn_body(i, carry):
        @pl.when(i < chunks)
        def _():
            begin(i)

        @pl.when((i == 1) & (section == 0))
        def _():
            for micro in range(1, n_section):
                keep(micro)
                for hop in range(1, n_dp):
                    deliver(micro, hop).start()

        @pl.when(i == LAG)
        def _():
            for idx in range(n_mp):
                load_weight(idx).wait()

        t = i - LAG

        @pl.when(t >= 0)
        def _():
            share(t)
            multiply(t)

        return carry

    lax.fori_loop(0, chunks + LAG, turn_body, 0)

    @pl.when(section < last)
    def _():
        for half in range(per_micro):
            bring_home(half).wait_recv()

    for chip_pos in range(n_ring):
        w_out_other(chip_pos).wait_send()
    swap.wait_send()
    for h in range(2):
        for kind in range(3):
            if kind != FAR:
                for p in range(PARTS):
                    rs1(h, kind, p, 1).wait_send()
            rs2(h, kind).wait_send()

    @pl.when(section == 0)
    def _():
        for micro in range(n_section):
            for hop in range(1, n_dp):
                deliver(micro, hop).wait_send()

    @pl.when(section != 0)
    def _():
        feed().wait_send()
        for micro in range(paced, n_section):
            delivered(micro)

    def settle(t, carry):
        for slot in range(3):
            shard_copy(t, 1, slot).wait_send()
        lend(t).wait_send()

        @pl.when((section < last) | (t < last * per_micro))
        def _():
            entry(t).wait_send()

        return carry

    lax.fori_loop(0, chunks, settle, 0)


def per_device(
    n_section,
    n_dp,
    n_mp,
    patches,
    ln_gain,
    ln_bias,
    w_merge_in,
    b_merge_in,
    w_merge_out,
    b_merge_out,
    text_rows,
    section_gain,
    section_weight,
    image_sizes,
    placement,
    offsets,
):
    rows_enc, inner = patches.shape
    depth, features_out = w_merge_out.shape
    seq_len, width = text_rows.shape[2:]
    n_ring = n_mp // 2
    sub = width // n_section
    half = rows_enc // 2
    chunks = n_section * seq_len // ROWS
    per_micro = seq_len // ROWS
    slots = n_section * n_dp * K_PAIR * SLOT
    dma = pltpu.SemaphoreType.DMA
    vmem = pl.BlockSpec(memory_space=pltpu.VMEM)
    hbm = pl.BlockSpec(memory_space=pl.ANY)
    out = pl.pallas_call(
        kernel,
        out_shape=jax.ShapeDtypeStruct((seq_len, width), BF16),
        in_specs=[hbm, vmem, vmem, hbm, vmem, hbm, vmem, vmem, vmem, hbm, vmem, vmem, vmem],
        out_specs=vmem,
        scratch_shapes=[
            pltpu.VMEM((rows_enc, inner), BF16),
            pltpu.VMEM((rows_enc, inner), BF16),
            pltpu.VMEM((depth, inner), BF16),
            pltpu.VMEM((2, n_ring, depth, width), BF16),
            pltpu.VMEM((n_ring, depth, width), BF16),
            pltpu.VMEM((2, rows_enc, depth), BF16),
            pltpu.VMEM((2, 3, PARTS, half, width // PARTS), BF16),
            pltpu.VMEM((2, 3, PARTS, half, width // PARTS), BF16),
            pltpu.VMEM((2, 3, half, sub), BF16),
            pltpu.VMEM((2, 3, half, sub), BF16),
            pltpu.VMEM((2, half, width), F32),
            pltpu.VMEM((rows_enc, sub), BF16),
            pltpu.VMEM((slots, rows_enc), BF16),
            pltpu.VMEM((slots, sub), BF16),
            pltpu.VMEM((n_section, seq_len, width), BF16),
            pltpu.VMEM((seq_len, width), BF16),
            pltpu.VMEM((n_section, seq_len, width), BF16),
            pltpu.VMEM((chunks, 2, n_ring, ROWS, width), BF16),
            pltpu.VMEM((n_mp, width, width), BF16),
            pltpu.VMEM((n_mp, TALL, width), BF16),
            pltpu.VMEM((ROWS, width), F32),
            pltpu.VMEM((ROWS, 128), F32),
            pltpu.VMEM((chunks, ROWS, width), BF16),
            dma((2,)),
            dma((4, n_ring)),
            dma((2,)),
            dma((2, 3, PARTS)),
            dma((2, 3, PARTS)),
            dma((2, 3)),
            dma((2, 3)),
            dma,
            dma((n_section,)),
            dma((n_section, n_dp)),
            dma((chunks,)),
            dma((n_mp,)),
            dma((chunks, 5)),
            dma((chunks, 5)),
            dma((per_micro,)),
        ],
        compiler_params=pltpu.CompilerParams(
            collective_id=0, has_side_effects=True, vmem_limit_bytes=60 * 2**20
        ),
    )(
        patches,
        ln_gain.reshape(-1, 128),
        ln_bias.reshape(-1, 128),
        w_merge_in.T,
        b_merge_in.reshape(1, -1),
        w_merge_out,
        b_merge_out.reshape(-1, 128),
        text_rows.reshape(seq_len, width),
        section_gain,
        section_weight.reshape(n_mp, width, width),
        image_sizes,
        placement,
        offsets,
    )
    return out.reshape(1, 1, seq_len, width)


def solution(mesh):
    in_specs = (
        P("dp", None),
        P(),
        P(),
        P(None, ("section", "mp")),
        P(("section", "mp")),
        P(("section", "mp"), None),
        P(),
        P("section", "dp", None, "mp"),
        P("section", None),
        P("section", None, "mp"),
        P(),
        P(),
        P(),
    )
    out_specs = P("section", "dp", None, "mp")
    sizes = (mesh.shape["section"], mesh.shape["dp"], mesh.shape["mp"])

    def run(*arrays):
        return per_device(*sizes, *arrays)

    return jax.shard_map(run, mesh=mesh, in_specs=in_specs, out_specs=out_specs, check_vma=False)
```

```python
import jax
import jax.numpy as jnp
from jax import lax
from jax.experimental import pallas as pl
from jax.experimental.pallas import tpu as pltpu
from jax.sharding import PartitionSpec as P

SLOT = 8
K_PAIR = 4
ROWS = 32
TALL = 128
LAG = 2
PARTS = 2
MESH = pl.DeviceIdType.MESH
F32 = jnp.float32
BF16 = jnp.bfloat16


def place(slots, sizes, places, starts_at):
    count = sizes.shape[1]
    images = lax.broadcasted_iota(jnp.int32, (slots.shape[0], count), 1)
    match = places == slots // SLOT

    def picked(values):
        return jnp.sum(jnp.where(match, values, 0), axis=1, keepdims=True)

    image = picked(images)
    extent = picked(sizes)
    first = jnp.sum(jnp.where(images < image, sizes, 0), axis=1, keepdims=True)
    column = lax.rem(slots, SLOT) - jnp.minimum(picked(starts_at), SLOT - extent)
    return first + column, (column >= 0) & (column < extent)


def kernel(
    patches_hbm, ln_gain_ref, ln_bias_ref, w_in_hbm, b_in_ref, w_out_hbm, b_out_ref, text_ref,
    gain_ref, weight_hbm, sizes_ref, places_ref, offsets_ref,
    out_ref,
    patches, encoded, w_in, w_out, w_lent, hidden, out1, in1, out2, in2, own, piece, picks, placed, images, text, texts,
    shards, weight, tall, total, squares, results,
    load_sem, w_out_sem, hid_sem, rs1_sent, rs1_got, rs2_sent, rs2_got, text_sent, text_got, place_sent, image_got,
    weight_sem, got, sent, home_sem,
):
    section, dp, mp = (lax.axis_index(a) for a in ("section", "dp", "mp"))
    n_section, n_dp, n_mp = (lax.axis_size(a) for a in ("section", "dp", "mp"))
    n_ring = n_mp // 2
    chip, core = mp // 2, lax.rem(mp, 2)
    chunks, _, _, rows, width = shards.shape
    per_micro = chunks // n_section
    seq_len = rows * per_micro
    per_group = K_PAIR * SLOT
    rows_enc, inner = patches.shape
    features = ln_gain_ref.shape[0] * 128
    half_rows = rows_enc // 2
    sub = width // n_section
    span = width // PARTS

    def at(chip_pos, core_pos):
        return lax.rem(chip_pos + n_ring, n_ring) * 2 + core_pos

    ahead, behind = at(chip + 1, core), at(chip - 1, core)
    sibling = at(chip, 1 - core)
    turn = 1 - 2 * core

    def load(src, dst, slot):
        return pltpu.make_async_copy(src, dst, load_sem.at[slot])

    def load_weight(idx):
        return pltpu.make_async_copy(weight_hbm.at[idx], weight.at[idx], weight_sem.at[idx])

    barrier = pltpu.get_barrier_semaphore()

    def greet(**target):
        pl.semaphore_signal(barrier, inc=1, device_id=target, device_id_type=MESH)

    load(patches_hbm, patches, 1).start()
    load(w_in_hbm, w_in, 0).start()
    for partner in (ahead, behind, sibling):
        greet(mp=partner)

    @pl.when(section == 0)
    def _():
        for there in range(n_section):
            for hop in range(n_dp):
                if there or hop:
                    greet(section=there, dp=lax.rem(dp + hop, n_dp))

    @pl.when(section != 0)
    def _():
        for hop in range(n_dp):
            greet(section=0, dp=lax.rem(dp + hop, n_dp))
        for hop in range(1, n_section):
            there = lax.rem(section + hop, n_section)

            @pl.when(there != 0)
            def _():
                greet(section=there)

    def w_out_block(chip_pos, core_pos):
        columns = pl.multiple_of((chip_pos * 2 + core_pos) * width, width)
        return w_out_hbm.at[:, pl.ds(columns, width)]

    def w_out_own(chip_pos):
        return pltpu.make_async_copy(w_out_block(chip_pos, core), w_out.at[0, chip_pos], w_out_sem.at[0, chip_pos])

    def w_out_fetch(chip_pos):
        return pltpu.make_async_copy(w_out_block(chip_pos, 1 - core), w_lent.at[chip_pos], w_out_sem.at[3, chip_pos])

    def w_out_other(chip_pos):
        return pltpu.make_async_remote_copy(
            src_ref=w_lent.at[chip_pos], dst_ref=w_out.at[1, chip_pos],
            send_sem=w_out_sem.at[1, chip_pos], recv_sem=w_out_sem.at[2, chip_pos],
            device_id={"mp": sibling}, device_id_type=MESH,
        )

    for chip_pos in range(n_ring):
        w_out_fetch(chip_pos).start()
    for chip_pos in range(n_ring):
        w_out_own(chip_pos).start()

    def one_row(ref, begin, count):
        return jnp.concatenate([ref[pl.ds(begin + k, 1), :] for k in range(count)], axis=1)

    ln_gain = one_row(ln_gain_ref, 0, features // 128)
    ln_bias = one_row(ln_bias_ref, 0, features // 128)
    load(patches_hbm, patches, 1).wait()
    block = 16

    def norm(b, carry):
        here = pl.ds(pl.multiple_of(b * block, block), block)
        for q in range(inner // features):
            columns = slice(q * features, (q + 1) * features)
            values = patches[here, columns].astype(F32)
            centre = values - jnp.mean(values, axis=-1, keepdims=True)
            spread = jnp.mean(centre * centre, axis=-1, keepdims=True)
            normed = centre * lax.rsqrt(spread + 1e-06) * ln_gain + ln_bias
            encoded[here, columns] = normed.astype(BF16)
        return carry

    lax.fori_loop(0, rows_enc // block, norm, 0)
    pl.semaphore_wait(barrier, jnp.where(section == 0, n_section * n_dp + 2, n_dp + n_section + 1))

    for chip_pos in range(n_ring):
        w_out_fetch(chip_pos).wait()
        w_out_other(chip_pos).start()

    load(w_in_hbm, w_in, 0).wait()
    before = lax.dot_general(
        encoded[...], w_in[...], (((1,), (1,)), ((), ())), preferred_element_type=F32
    ) + b_in_ref[...]
    hidden[0] = (0.5 * before * (1.0 + lax.erf(before * (0.5**0.5)))).astype(BF16)

    swap = pltpu.make_async_remote_copy(
        src_ref=hidden.at[0], dst_ref=hidden.at[1], send_sem=hid_sem.at[0], recv_sem=hid_sem.at[1],
        device_id={"mp": sibling}, device_id_type=MESH,
    )
    swap.start()
    for chip_pos in range(n_ring):
        w_out_own(chip_pos).wait()
    for chip_pos in range(n_ring):
        w_out_other(chip_pos).wait_recv()
    swap.wait_recv()

    def along(axis, delta):
        if axis:
            return {"section": lax.rem(section + delta + n_section, n_section)}
        return {"mp": at(chip + delta, core)}

    def spot(axis, delta):
        return lax.rem((section if axis else chip) + delta + n_ring, n_ring)

    def partial(h, idx, p):
        def product(k, chip_pos, columns):
            return jnp.dot(
                hidden[k, h * half_rows : (h + 1) * half_rows, :], w_out[k, chip_pos, :, columns],
                preferred_element_type=F32,
            )

        if h == 0:
            columns = slice(p * span, (p + 1) * span)
            return product(0, idx, columns) + product(1, idx, columns)
        columns = pl.ds(pl.multiple_of(idx * sub, sub), sub)
        count = span // sub
        return jnp.concatenate(
            [product(0, z, columns) + product(1, z, columns) for z in range(p * count, (p + 1) * count)], axis=1
        )

    def rs1(h, kind, p, delta):
        return pltpu.make_async_remote_copy(
            src_ref=out1.at[h, kind, p], dst_ref=in1.at[h, kind, p],
            send_sem=rs1_sent.at[h, kind, p], recv_sem=rs1_got.at[h, kind, p],
            device_id=along(h, delta), device_id_type=MESH,
        )

    def rs2(h, kind):
        return pltpu.make_async_remote_copy(
            src_ref=out2.at[h, kind], dst_ref=in2.at[h, kind],
            send_sem=rs2_sent.at[h, kind], recv_sem=rs2_got.at[h, kind],
            device_id=along(1 - h, kind + 1), device_id_type=MESH,
        )

    FAR, NEAR, SUM = 0, 1, 2
    for p in range(PARTS):
        for h in range(2):
            out1[h, FAR, p] = partial(h, spot(h, 2), p).astype(BF16)
            rs1(h, FAR, p, turn).start()
    for p in range(PARTS):
        for h in range(2):
            out1[h, NEAR, p] = partial(h, spot(h, -turn), p).astype(BF16)
            rs1(h, FAR, p, turn).wait_send()
            rs1(h, NEAR, p, -turn).start()
    for p in range(PARTS):
        for h in range(2):
            value = partial(h, spot(h, turn), p)
            rs1(h, FAR, p, turn).wait_recv()
            out1[h, SUM, p] = (value + in1[h, FAR, p].astype(F32)).astype(BF16)
            rs1(h, SUM, p, turn).start()
    for p in range(PARTS):
        for h in range(2):
            own[h, :, p * span : (p + 1) * span] = partial(h, spot(h, 0), p)

    for idx in range(n_mp):
        load_weight(idx).start()

    tall[...] = jnp.zeros_like(tall)

    position = lax.broadcasted_iota(jnp.int32, (seq_len, 1), 0)
    group = position // per_group
    owner = section * n_dp + dp
    slots = owner * per_group + lax.rem(position, per_group)

    def by_group(ref):
        values = jnp.broadcast_to(ref[0:1, :], (seq_len, ref.shape[1]))
        for e in range(1, n_dp):
            values = jnp.where(group == e, ref[e : e + 1, :], values)
        return values

    _, covered = place(slots, by_group(sizes_ref), by_group(places_ref), by_group(offsets_ref))
    text[...] = jnp.where(covered, jnp.zeros((), F32), text_ref[...].astype(F32)).astype(BF16)

    everywhere = lax.broadcasted_iota(jnp.int32, (n_section * n_dp * per_group, 1), 0)
    mine = pl.ds(dp, 1)
    row, covered = place(everywhere, sizes_ref[mine, :], places_ref[mine, :], offsets_ref[mine, :])
    candidates = lax.broadcasted_iota(jnp.int32, (everywhere.shape[0], rows_enc), 1)
    picks[...] = jnp.where((candidates == row) & covered, 1.0, 0.0).astype(BF16)

    for p in range(PARTS):
        for h in range(2):
            columns = slice(p * span, (p + 1) * span)
            rs1(h, NEAR, p, -turn).wait_recv()
            rs1(h, SUM, p, turn).wait_recv()
            own[h, :, columns] += in1[h, NEAR, p].astype(F32) + in1[h, SUM, p].astype(F32)

    def own_block(h, delta):
        columns = pl.ds(pl.multiple_of(spot(1 - h, delta) * sub, sub), sub)
        return own[h, :, columns]

    for kind in (1, 0, 2):
        for h in range(2):
            out2[h, kind] = own_block(h, kind + 1).astype(BF16)
            rs2(h, kind).start()
    bias = one_row(b_out_ref, (mp * n_section + section) * (sub // 128), sub // 128)
    for h in range(2):
        value = own_block(h, 0) + bias
        for kind in (0, 2, 1):
            rs2(h, kind).wait_recv()
            value = value + in2[h, kind].astype(F32)
        piece[h * half_rows : (h + 1) * half_rows, :] = value.astype(BF16)

    placed[...] = jnp.dot(picks[...], piece[...], preferred_element_type=F32).astype(BF16)

    def block_of(micro, seq):
        begin = pl.multiple_of((micro * n_dp + seq) * per_group, per_group)
        return placed.at[pl.ds(begin, per_group)]

    def landing(micro):
        return images.at[
            micro, pl.ds(pl.multiple_of(dp * per_group, per_group), per_group),
            pl.ds(pl.multiple_of(section * sub, sub), sub),
        ]

    part_of = dp * per_group // rows

    def deliver(micro, hop):
        seq = lax.rem(dp + hop, n_dp)
        return pltpu.make_async_remote_copy(
            src_ref=block_of(micro, seq), dst_ref=landing(micro),
            send_sem=place_sent.at[micro, hop], recv_sem=image_got.at[micro * per_micro + part_of],
            device_id={"section": 0, "dp": seq}, device_id_type=MESH,
        )

    def feed():
        return pltpu.make_async_remote_copy(
            src_ref=text, dst_ref=texts.at[section],
            send_sem=text_sent, recv_sem=text_got.at[section],
            device_id={"section": 0}, device_id_type=MESH,
        )

    def keep(micro):
        pltpu.make_async_copy(
            block_of(micro, dp), landing(micro), image_got.at[micro * per_micro + part_of]
        ).start()

    def deliver_all(micro):
        for hop in range(n_dp):
            deliver(micro, hop).start()

    def delivered(micro):
        for hop in range(n_dp):
            deliver(micro, hop).wait_send()

    paced = 2

    @pl.when(section == 0)
    def _():
        pltpu.make_async_copy(text, texts.at[0], text_got.at[0]).start()
        keep(0)
        for hop in range(1, n_dp):
            deliver(0, hop).start()

    @pl.when(section != 0)
    def _():
        for micro in range(n_section):
            if micro:
                @pl.when(section == micro)
                def _():
                    feed().start()

            deliver_all(micro)
            if micro < paced:
                delivered(micro)

    def ring(step):
        return lax.rem(chip + step * turn + n_ring, n_ring)

    def shard_copy(t, step, slot):
        return pltpu.make_async_remote_copy(
            src_ref=shards.at[t, core, chip], dst_ref=shards.at[t, core, chip],
            send_sem=sent.at[t, slot], recv_sem=got.at[t, slot],
            device_id={"mp": at(chip + step * turn, core)}, device_id_type=MESH,
        )

    def entry(t):
        return pltpu.make_async_remote_copy(
            src_ref=results.at[t], dst_ref=shards.at[t, core, chip],
            send_sem=sent.at[t, 4], recv_sem=got.at[t, 4],
            device_id={"section": lax.rem(section + 1, n_section)}, device_id_type=MESH,
        )

    def lend(t):
        return pltpu.make_async_remote_copy(
            src_ref=shards.at[t, core], dst_ref=shards.at[t, core],
            send_sem=sent.at[t, 3], recv_sem=got.at[t, 3],
            device_id={"mp": sibling}, device_id_type=MESH,
        )

    def enter(t):
        micro, part = t // per_micro, lax.rem(t, per_micro)
        here = pl.ds(pl.multiple_of(part * rows, rows), rows)

        @pl.when(part == 0)
        def _():
            pltpu.make_async_remote_copy(
                src_ref=text, dst_ref=texts.at[micro], send_sem=text_sent, recv_sem=text_got.at[micro],
                device_id={"section": 0}, device_id_type=MESH,
            ).wait_recv()

        pltpu.make_async_remote_copy(
            src_ref=images.at[micro, here], dst_ref=images.at[micro, here],
            send_sem=text_sent, recv_sem=image_got.at[t],
            device_id={"section": 0}, device_id_type=MESH,
        ).wait_recv()
        shards[t, core, chip] = (images[micro, here, :].astype(F32) + texts[micro, here, :].astype(F32)).astype(BF16)

    def bring_home(t):
        half = lax.rem(t, per_micro)
        return pltpu.make_async_remote_copy(
            src_ref=results.at[t], dst_ref=out_ref.at[pl.ds(pl.multiple_of(half * rows, rows), rows)],
            send_sem=sent.at[t, 4], recv_sem=home_sem.at[half],
            device_id={"section": t // per_micro}, device_id_type=MESH,
        )

    def add(t, core_pos, chip_pos, first=False):
        idx = chip_pos * 2 + core_pos
        values = shards[t, core_pos, chip_pos].astype(F32)
        square = values * values
        lanes = square[:, :128] if first else squares[...] + square[:, :128]
        for j in range(128, width, 128):
            lanes = lanes + square[:, j : j + 128]
        squares[...] = lanes
        gain = gain_ref[:, pl.ds(pl.multiple_of(idx * width, width), width)]
        tall[idx, 0:rows] = (values * gain).astype(BF16)
        update = jnp.dot(tall[idx], weight[idx], preferred_element_type=F32)[0:rows]
        total[...] = update if first else total[...] + update

    last = n_section - 1
    def begin(t):
        @pl.when(section == 0)
        def _():
            enter(t)

        @pl.when(section != 0)
        def _():
            entry(t).wait_recv()

        shard_copy(t, 1, 0).start()
        shard_copy(t, -1, 1).start()
        shard_copy(t, 2, 2).start()

    def share(t):
        for slot in range(3):
            shard_copy(t, 1, slot).wait_recv()
        lend(t).start()

    def multiply(t):
        for step in range(n_ring):
            add(t, core, ring(step), step == 0)
        lend(t).wait_recv()
        for step in range(n_ring):
            add(t, 1 - core, ring(step))
        square = jnp.sum(squares[...], axis=-1, keepdims=True) * (1.0 / (n_mp * width))
        update = total[...] * lax.rsqrt(square + 1e-06)
        result = (shards[t, core, chip].astype(F32) + update).astype(BF16)
        results[t] = result

        @pl.when(section < last)
        def _():
            entry(t).start()

        @pl.when((section == last) & (t < last * per_micro))
        def _():
            bring_home(t).start()

        @pl.when((section == last) & (t >= last * per_micro))
        def _():
            part = lax.rem(t, per_micro)
            out_ref[pl.ds(pl.multiple_of(part * rows, rows), rows)] = result

    def turn_body(i, carry):
        @pl.when(i < chunks)
        def _():
            begin(i)

        @pl.when((i == 1) & (section == 0))
        def _():
            for micro in range(1, n_section):
                keep(micro)
                for hop in range(1, n_dp):
                    deliver(micro, hop).start()

        @pl.when(i == LAG)
        def _():
            for idx in range(n_mp):
                load_weight(idx).wait()

        t = i - LAG

        @pl.when(t >= 0)
        def _():
            share(t)
            multiply(t)

        return carry

    lax.fori_loop(0, chunks + LAG, turn_body, 0)

    @pl.when(section < last)
    def _():
        for half in range(per_micro):
            bring_home(half).wait_recv()

    for chip_pos in range(n_ring):
        w_out_other(chip_pos).wait_send()
    swap.wait_send()
    for h in range(2):
        for kind in range(3):
            if kind != FAR:
                for p in range(PARTS):
                    rs1(h, kind, p, 1).wait_send()
            rs2(h, kind).wait_send()

    @pl.when(section == 0)
    def _():
        for micro in range(n_section):
            for hop in range(1, n_dp):
                deliver(micro, hop).wait_send()

    @pl.when(section != 0)
    def _():
        feed().wait_send()
        for micro in range(paced, n_section):
            delivered(micro)

    def settle(t, carry):
        for slot in range(3):
            shard_copy(t, 1, slot).wait_send()
        lend(t).wait_send()

        @pl.when((section < last) | (t < last * per_micro))
        def _():
            entry(t).wait_send()

        return carry

    lax.fori_loop(0, chunks, settle, 0)


def per_device(
    n_section,
    n_dp,
    n_mp,
    patches,
    ln_gain,
    ln_bias,
    w_merge_in,
    b_merge_in,
    w_merge_out,
    b_merge_out,
    text_rows,
    section_gain,
    section_weight,
    image_sizes,
    placement,
    offsets,
):
    rows_enc, inner = patches.shape
    depth, features_out = w_merge_out.shape
    seq_len, width = text_rows.shape[2:]
    n_ring = n_mp // 2
    sub = width // n_section
    half = rows_enc // 2
    chunks = n_section * seq_len // ROWS
    per_micro = seq_len // ROWS
    slots = n_section * n_dp * K_PAIR * SLOT
    dma = pltpu.SemaphoreType.DMA
    vmem = pl.BlockSpec(memory_space=pltpu.VMEM)
    hbm = pl.BlockSpec(memory_space=pl.ANY)
    out = pl.pallas_call(
        kernel,
        out_shape=jax.ShapeDtypeStruct((seq_len, width), BF16),
        in_specs=[hbm, vmem, vmem, hbm, vmem, hbm, vmem, vmem, vmem, hbm, vmem, vmem, vmem],
        out_specs=vmem,
        scratch_shapes=[
            pltpu.VMEM((rows_enc, inner), BF16),
            pltpu.VMEM((rows_enc, inner), BF16),
            pltpu.VMEM((depth, inner), BF16),
            pltpu.VMEM((2, n_ring, depth, width), BF16),
            pltpu.VMEM((n_ring, depth, width), BF16),
            pltpu.VMEM((2, rows_enc, depth), BF16),
            pltpu.VMEM((2, 3, PARTS, half, width // PARTS), BF16),
            pltpu.VMEM((2, 3, PARTS, half, width // PARTS), BF16),
            pltpu.VMEM((2, 3, half, sub), BF16),
            pltpu.VMEM((2, 3, half, sub), BF16),
            pltpu.VMEM((2, half, width), F32),
            pltpu.VMEM((rows_enc, sub), BF16),
            pltpu.VMEM((slots, rows_enc), BF16),
            pltpu.VMEM((slots, sub), BF16),
            pltpu.VMEM((n_section, seq_len, width), BF16),
            pltpu.VMEM((seq_len, width), BF16),
            pltpu.VMEM((n_section, seq_len, width), BF16),
            pltpu.VMEM((chunks, 2, n_ring, ROWS, width), BF16),
            pltpu.VMEM((n_mp, width, width), BF16),
            pltpu.VMEM((n_mp, TALL, width), BF16),
            pltpu.VMEM((ROWS, width), F32),
            pltpu.VMEM((ROWS, 128), F32),
            pltpu.VMEM((chunks, ROWS, width), BF16),
            dma((2,)),
            dma((4, n_ring)),
            dma((2,)),
            dma((2, 3, PARTS)),
            dma((2, 3, PARTS)),
            dma((2, 3)),
            dma((2, 3)),
            dma,
            dma((n_section,)),
            dma((n_section, n_dp)),
            dma((chunks,)),
            dma((n_mp,)),
            dma((chunks, 5)),
            dma((chunks, 5)),
            dma((per_micro,)),
        ],
        compiler_params=pltpu.CompilerParams(
            collective_id=0, has_side_effects=True, vmem_limit_bytes=60 * 2**20
        ),
    )(
        patches,
        ln_gain.reshape(-1, 128),
        ln_bias.reshape(-1, 128),
        w_merge_in.T,
        b_merge_in.reshape(1, -1),
        w_merge_out,
        b_merge_out.reshape(-1, 128),
        text_rows.reshape(seq_len, width),
        section_gain,
        section_weight.reshape(n_mp, width, width),
        image_sizes,
        placement,
        offsets,
    )
    return out.reshape(1, 1, seq_len, width)


def solution(mesh):
    in_specs = (
        P("dp", None),
        P(),
        P(),
        P(None, ("section", "mp")),
        P(("section", "mp")),
        P(("section", "mp"), None),
        P(),
        P("section", "dp", None, "mp"),
        P("section", None),
        P("section", None, "mp"),
        P(),
        P(),
        P(),
    )
    out_specs = P("section", "dp", None, "mp")
    sizes = (mesh.shape["section"], mesh.shape["dp"], mesh.shape["mp"])

    def run(*arrays):
        return per_device(*sizes, *arrays)

    return jax.shard_map(run, mesh=mesh, in_specs=in_specs, out_specs=out_specs, check_vma=False)
```

```python
import jax
import jax.numpy as jnp
from jax import lax
from jax.experimental import pallas as pl
from jax.experimental.pallas import tpu as pltpu
from jax.sharding import PartitionSpec as P

SLOT = 8
K_PAIR = 4
ROWS = 32
TALL = 128
LAG = 2
PARTS = 2
MESH = pl.DeviceIdType.MESH
F32 = jnp.float32
BF16 = jnp.bfloat16


def place(slots, sizes, places, starts_at):
    count = sizes.shape[1]
    images = lax.broadcasted_iota(jnp.int32, (slots.shape[0], count), 1)
    match = places == slots // SLOT

    def picked(values):
        return jnp.sum(jnp.where(match, values, 0), axis=1, keepdims=True)

    image = picked(images)
    extent = picked(sizes)
    first = jnp.sum(jnp.where(images < image, sizes, 0), axis=1, keepdims=True)
    column = lax.rem(slots, SLOT) - jnp.minimum(picked(starts_at), SLOT - extent)
    return first + column, (column >= 0) & (column < extent)


def kernel(
    patches_hbm, ln_gain_ref, ln_bias_ref, w_in_hbm, b_in_ref, w_out_hbm, b_out_ref, text_ref,
    gain_ref, weight_hbm, sizes_ref, places_ref, offsets_ref,
    out_ref,
    patches, encoded, w_in, w_out, w_lent, hidden, out1, in1, out2, in2, own, piece, picks, placed, images, text, texts,
    shards, weight, tall, total, squares, results,
    load_sem, w_out_sem, hid_sem, rs1_sent, rs1_got, rs2_sent, rs2_got, text_sent, text_got, place_sent, image_got,
    weight_sem, got, sent, home_sem,
):
    section, dp, mp = (lax.axis_index(a) for a in ("section", "dp", "mp"))
    n_section, n_dp, n_mp = (lax.axis_size(a) for a in ("section", "dp", "mp"))
    n_ring = n_mp // 2
    chip, core = mp // 2, lax.rem(mp, 2)
    chunks, _, _, rows, width = shards.shape
    per_micro = chunks // n_section
    seq_len = rows * per_micro
    per_group = K_PAIR * SLOT
    rows_enc, inner = patches.shape
    features = ln_gain_ref.shape[0] * 128
    half_rows = rows_enc // 2
    sub = width // n_section
    span = width // PARTS

    def at(chip_pos, core_pos):
        return lax.rem(chip_pos + n_ring, n_ring) * 2 + core_pos

    ahead, behind = at(chip + 1, core), at(chip - 1, core)
    sibling = at(chip, 1 - core)
    turn = 1 - 2 * core

    def load(src, dst, slot):
        return pltpu.make_async_copy(src, dst, load_sem.at[slot])

    def load_weight(idx):
        return pltpu.make_async_copy(weight_hbm.at[idx], weight.at[idx], weight_sem.at[idx])

    barrier = pltpu.get_barrier_semaphore()

    def greet(**target):
        pl.semaphore_signal(barrier, inc=1, device_id=target, device_id_type=MESH)

    load(patches_hbm, patches, 1).start()
    load(w_in_hbm, w_in, 0).start()
    for partner in (ahead, behind, sibling):
        greet(mp=partner)

    @pl.when(section == 0)
    def _():
        for there in range(n_section):
            for hop in range(n_dp):
                if there or hop:
                    greet(section=there, dp=lax.rem(dp + hop, n_dp))

    @pl.when(section != 0)
    def _():
        for hop in range(n_dp):
            greet(section=0, dp=lax.rem(dp + hop, n_dp))
        for hop in range(1, n_section):
            there = lax.rem(section + hop, n_section)

            @pl.when(there != 0)
            def _():
                greet(section=there)

    def w_out_block(chip_pos, core_pos):
        columns = pl.multiple_of((chip_pos * 2 + core_pos) * width, width)
        return w_out_hbm.at[:, pl.ds(columns, width)]

    def w_out_own(chip_pos):
        return pltpu.make_async_copy(w_out_block(chip_pos, core), w_out.at[0, chip_pos], w_out_sem.at[0, chip_pos])

    def w_out_fetch(chip_pos):
        return pltpu.make_async_copy(w_out_block(chip_pos, 1 - core), w_lent.at[chip_pos], w_out_sem.at[3, chip_pos])

    def w_out_other(chip_pos):
        return pltpu.make_async_remote_copy(
            src_ref=w_lent.at[chip_pos], dst_ref=w_out.at[1, chip_pos],
            send_sem=w_out_sem.at[1, chip_pos], recv_sem=w_out_sem.at[2, chip_pos],
            device_id={"mp": sibling}, device_id_type=MESH,
        )

    for chip_pos in range(n_ring):
        w_out_fetch(chip_pos).start()
    for chip_pos in range(n_ring):
        w_out_own(chip_pos).start()

    def one_row(ref, begin, count):
        return jnp.concatenate([ref[pl.ds(begin + k, 1), :] for k in range(count)], axis=1)

    ln_gain = one_row(ln_gain_ref, 0, features // 128)
    ln_bias = one_row(ln_bias_ref, 0, features // 128)
    load(patches_hbm, patches, 1).wait()
    block = 16

    def norm(b, carry):
        here = pl.ds(pl.multiple_of(b * block, block), block)
        for q in range(inner // features):
            columns = slice(q * features, (q + 1) * features)
            values = patches[here, columns].astype(F32)
            centre = values - jnp.mean(values, axis=-1, keepdims=True)
            spread = jnp.mean(centre * centre, axis=-1, keepdims=True)
            normed = centre * lax.rsqrt(spread + 1e-06) * ln_gain + ln_bias
            encoded[here, columns] = normed.astype(BF16)
        return carry

    lax.fori_loop(0, rows_enc // block, norm, 0)
    pl.semaphore_wait(barrier, jnp.where(section == 0, n_section * n_dp + 2, n_dp + n_section + 1))

    for chip_pos in range(n_ring):
        w_out_fetch(chip_pos).wait()
        w_out_other(chip_pos).start()

    load(w_in_hbm, w_in, 0).wait()
    before = lax.dot_general(
        encoded[...], w_in[...], (((1,), (1,)), ((), ())), preferred_element_type=F32
    ) + b_in_ref[...]
    hidden[0] = (0.5 * before * (1.0 + lax.erf(before * (0.5**0.5)))).astype(BF16)

    swap = pltpu.make_async_remote_copy(
        src_ref=hidden.at[0], dst_ref=hidden.at[1], send_sem=hid_sem.at[0], recv_sem=hid_sem.at[1],
        device_id={"mp": sibling}, device_id_type=MESH,
    )
    swap.start()
    for chip_pos in range(n_ring):
        w_out_own(chip_pos).wait()
    for chip_pos in range(n_ring):
        w_out_other(chip_pos).wait_recv()
    swap.wait_recv()

    def along(axis, delta):
        if axis:
            return {"section": lax.rem(section + delta + n_section, n_section)}
        return {"mp": at(chip + delta, core)}

    def spot(axis, delta):
        return lax.rem((section if axis else chip) + delta + n_ring, n_ring)

    def partial(h, idx, p):
        def product(k, chip_pos, columns):
            return jnp.dot(
                hidden[k, h * half_rows : (h + 1) * half_rows, :], w_out[k, chip_pos, :, columns],
                preferred_element_type=F32,
            )

        if h == 0:
            columns = slice(p * span, (p + 1) * span)
            return product(0, idx, columns) + product(1, idx, columns)
        columns = pl.ds(pl.multiple_of(idx * sub, sub), sub)
        count = span // sub
        return jnp.concatenate(
            [product(0, z, columns) + product(1, z, columns) for z in range(p * count, (p + 1) * count)], axis=1
        )

    def rs1(h, kind, p, delta):
        return pltpu.make_async_remote_copy(
            src_ref=out1.at[h, kind, p], dst_ref=in1.at[h, kind, p],
            send_sem=rs1_sent.at[h, kind, p], recv_sem=rs1_got.at[h, kind, p],
            device_id=along(h, delta), device_id_type=MESH,
        )

    def rs2(h, kind):
        return pltpu.make_async_remote_copy(
            src_ref=out2.at[h, kind], dst_ref=in2.at[h, kind],
            send_sem=rs2_sent.at[h, kind], recv_sem=rs2_got.at[h, kind],
            device_id=along(1 - h, kind + 1), device_id_type=MESH,
        )

    FAR, NEAR, SUM = 0, 1, 2
    for p in range(PARTS):
        for h in range(2):
            out1[h, FAR, p] = partial(h, spot(h, 2), p).astype(BF16)
            rs1(h, FAR, p, turn).start()
    for p in range(PARTS):
        for h in range(2):
            out1[h, NEAR, p] = partial(h, spot(h, -turn), p).astype(BF16)
            rs1(h, FAR, p, turn).wait_send()
            rs1(h, NEAR, p, -turn).start()
    for p in range(PARTS):
        for h in range(2):
            value = partial(h, spot(h, turn), p)
            rs1(h, FAR, p, turn).wait_recv()
            out1[h, SUM, p] = (value + in1[h, FAR, p].astype(F32)).astype(BF16)
            rs1(h, SUM, p, turn).start()
    for p in range(PARTS):
        for h in range(2):
            own[h, :, p * span : (p + 1) * span] = partial(h, spot(h, 0), p)

    for idx in range(n_mp):
        load_weight(idx).start()

    tall[...] = jnp.zeros_like(tall)

    position = lax.broadcasted_iota(jnp.int32, (seq_len, 1), 0)
    group = position // per_group
    owner = section * n_dp + dp
    slots = owner * per_group + lax.rem(position, per_group)

    def by_group(ref):
        values = jnp.broadcast_to(ref[0:1, :], (seq_len, ref.shape[1]))
        for e in range(1, n_dp):
            values = jnp.where(group == e, ref[e : e + 1, :], values)
        return values

    _, covered = place(slots, by_group(sizes_ref), by_group(places_ref), by_group(offsets_ref))
    text[...] = jnp.where(covered, jnp.zeros((), F32), text_ref[...].astype(F32)).astype(BF16)

    everywhere = lax.broadcasted_iota(jnp.int32, (n_section * n_dp * per_group, 1), 0)
    mine = pl.ds(dp, 1)
    row, covered = place(everywhere, sizes_ref[mine, :], places_ref[mine, :], offsets_ref[mine, :])
    candidates = lax.broadcasted_iota(jnp.int32, (everywhere.shape[0], rows_enc), 1)
    picks[...] = jnp.where((candidates == row) & covered, 1.0, 0.0).astype(BF16)

    for p in range(PARTS):
        for h in range(2):
            columns = slice(p * span, (p + 1) * span)
            rs1(h, NEAR, p, -turn).wait_recv()
            rs1(h, SUM, p, turn).wait_recv()
            own[h, :, columns] += in1[h, NEAR, p].astype(F32) + in1[h, SUM, p].astype(F32)

    def own_block(h, delta):
        columns = pl.ds(pl.multiple_of(spot(1 - h, delta) * sub, sub), sub)
        return own[h, :, columns]

    for kind in (1, 0, 2):
        for h in range(2):
            out2[h, kind] = own_block(h, kind + 1).astype(BF16)
            rs2(h, kind).start()
    bias = one_row(b_out_ref, (mp * n_section + section) * (sub // 128), sub // 128)
    for h in range(2):
        value = own_block(h, 0) + bias
        for kind in (0, 2, 1):
            rs2(h, kind).wait_recv()
            value = value + in2[h, kind].astype(F32)
        piece[h * half_rows : (h + 1) * half_rows, :] = value.astype(BF16)

    placed[...] = jnp.dot(picks[...], piece[...], preferred_element_type=F32).astype(BF16)

    def block_of(micro, seq):
        begin = pl.multiple_of((micro * n_dp + seq) * per_group, per_group)
        return placed.at[pl.ds(begin, per_group)]

    def landing(micro):
        return images.at[
            micro, pl.ds(pl.multiple_of(dp * per_group, per_group), per_group),
            pl.ds(pl.multiple_of(section * sub, sub), sub),
        ]

    part_of = dp * per_group // rows

    def deliver(micro, hop):
        seq = lax.rem(dp + hop, n_dp)
        return pltpu.make_async_remote_copy(
            src_ref=block_of(micro, seq), dst_ref=landing(micro),
            send_sem=place_sent.at[micro, hop], recv_sem=image_got.at[micro * per_micro + part_of],
            device_id={"section": 0, "dp": seq}, device_id_type=MESH,
        )

    def feed():
        return pltpu.make_async_remote_copy(
            src_ref=text, dst_ref=texts.at[section],
            send_sem=text_sent, recv_sem=text_got.at[section],
            device_id={"section": 0}, device_id_type=MESH,
        )

    def keep(micro):
        pltpu.make_async_copy(
            block_of(micro, dp), landing(micro), image_got.at[micro * per_micro + part_of]
        ).start()

    def deliver_all(micro):
        for hop in range(n_dp):
            deliver(micro, hop).start()

    def delivered(micro):
        for hop in range(n_dp):
            deliver(micro, hop).wait_send()

    paced = 2

    @pl.when(section == 0)
    def _():
        pltpu.make_async_copy(text, texts.at[0], text_got.at[0]).start()
        keep(0)
        for hop in range(1, n_dp):
            deliver(0, hop).start()

    @pl.when(section != 0)
    def _():
        for micro in range(n_section):
            if micro:
                @pl.when(section == micro)
                def _():
                    feed().start()

            deliver_all(micro)
            if micro < paced:
                delivered(micro)

    def ring(step):
        return lax.rem(chip + step * turn + n_ring, n_ring)

    def shard_copy(t, step, slot):
        return pltpu.make_async_remote_copy(
            src_ref=shards.at[t, core, 0], dst_ref=shards.at[t, core, slot + 1],
            send_sem=sent.at[t, slot], recv_sem=got.at[t, slot],
            device_id={"mp": at(chip + step * turn, core)}, device_id_type=MESH,
        )

    def entry(t):
        return pltpu.make_async_remote_copy(
            src_ref=results.at[t], dst_ref=shards.at[t, core, 0],
            send_sem=sent.at[t, 4], recv_sem=got.at[t, 4],
            device_id={"section": lax.rem(section + 1, n_section)}, device_id_type=MESH,
        )

    def lend(t, late):
        those = pl.ds(3, 1) if late else pl.ds(0, 3)
        slot = 5 if late else 3
        return pltpu.make_async_remote_copy(
            src_ref=shards.at[t, core, those], dst_ref=shards.at[t, core, those],
            send_sem=sent.at[t, slot], recv_sem=got.at[t, slot],
            device_id={"mp": sibling}, device_id_type=MESH,
        )

    def enter(t):
        micro, part = t // per_micro, lax.rem(t, per_micro)
        here = pl.ds(pl.multiple_of(part * rows, rows), rows)

        @pl.when(part == 0)
        def _():
            pltpu.make_async_remote_copy(
                src_ref=text, dst_ref=texts.at[micro], send_sem=text_sent, recv_sem=text_got.at[micro],
                device_id={"section": 0}, device_id_type=MESH,
            ).wait_recv()

        pltpu.make_async_remote_copy(
            src_ref=images.at[micro, here], dst_ref=images.at[micro, here],
            send_sem=text_sent, recv_sem=image_got.at[t],
            device_id={"section": 0}, device_id_type=MESH,
        ).wait_recv()
        shards[t, core, 0] = (images[micro, here, :].astype(F32) + texts[micro, here, :].astype(F32)).astype(BF16)

    def bring_home(t):
        half = lax.rem(t, per_micro)
        return pltpu.make_async_remote_copy(
            src_ref=results.at[t], dst_ref=out_ref.at[pl.ds(pl.multiple_of(half * rows, rows), rows)],
            send_sem=sent.at[t, 4], recv_sem=home_sem.at[half],
            device_id={"section": t // per_micro}, device_id_type=MESH,
        )

    def add(t, other, place):
        step = (0, 1, -1, 2)[place]
        core_pos = 1 - core if other else core
        idx = ring(step if other else -step) * 2 + core_pos
        first = not other and place == 0
        spare = place + 4 * other
        values = shards[t, core_pos, place].astype(F32)
        square = values * values
        lanes = square[:, :128] if first else squares[...] + square[:, :128]
        for j in range(128, width, 128):
            lanes = lanes + square[:, j : j + 128]
        squares[...] = lanes
        gain = gain_ref[:, pl.ds(pl.multiple_of(idx * width, width), width)]
        tall[spare, 0:rows] = (values * gain).astype(BF16)
        update = jnp.dot(tall[spare], weight[idx], preferred_element_type=F32)[0:rows]
        total[...] = update if first else total[...] + update

    last = n_section - 1
    def begin(t):
        @pl.when(section == 0)
        def _():
            enter(t)

        @pl.when(section != 0)
        def _():
            entry(t).wait_recv()

        shard_copy(t, 1, 0).start()
        shard_copy(t, -1, 1).start()
        shard_copy(t, 2, 2).start()

    def multiply(t):
        for slot in range(2):
            shard_copy(t, 1, slot).wait_recv()
        lend(t, 0).start()
        for place in range(3):
            add(t, 0, place)
        shard_copy(t, 1, 2).wait_recv()
        lend(t, 1).start()
        add(t, 0, 3)
        lend(t, 0).wait_recv()
        for place in range(3):
            add(t, 1, place)
        lend(t, 1).wait_recv()
        add(t, 1, 3)
        square = jnp.sum(squares[...], axis=-1, keepdims=True) * (1.0 / (n_mp * width))
        update = total[...] * lax.rsqrt(square + 1e-06)
        result = (shards[t, core, 0].astype(F32) + update).astype(BF16)
        results[t] = result

        @pl.when(section < last)
        def _():
            entry(t).start()

        @pl.when((section == last) & (t < last * per_micro))
        def _():
            bring_home(t).start()

        @pl.when((section == last) & (t >= last * per_micro))
        def _():
            part = lax.rem(t, per_micro)
            out_ref[pl.ds(pl.multiple_of(part * rows, rows), rows)] = result

    def turn_body(i, carry):
        @pl.when(i < chunks)
        def _():
            begin(i)

        @pl.when((i == 1) & (section == 0))
        def _():
            for micro in range(1, n_section):
                keep(micro)
                for hop in range(1, n_dp):
                    deliver(micro, hop).start()

        @pl.when(i == LAG)
        def _():
            for idx in range(n_mp):
                load_weight(idx).wait()

        t = i - LAG

        @pl.when(t >= 0)
        def _():
            multiply(t)

        return carry

    lax.fori_loop(0, chunks + LAG, turn_body, 0)

    @pl.when(section < last)
    def _():
        for half in range(per_micro):
            bring_home(half).wait_recv()

    for chip_pos in range(n_ring):
        w_out_other(chip_pos).wait_send()
    swap.wait_send()
    for h in range(2):
        for kind in range(3):
            if kind != FAR:
                for p in range(PARTS):
                    rs1(h, kind, p, 1).wait_send()
            rs2(h, kind).wait_send()

    @pl.when(section == 0)
    def _():
        for micro in range(n_section):
            for hop in range(1, n_dp):
                deliver(micro, hop).wait_send()

    @pl.when(section != 0)
    def _():
        feed().wait_send()
        for micro in range(paced, n_section):
            delivered(micro)

    def settle(t, carry):
        for slot in range(3):
            shard_copy(t, 1, slot).wait_send()
        for late in range(2):
            lend(t, late).wait_send()

        @pl.when((section < last) | (t < last * per_micro))
        def _():
            entry(t).wait_send()

        return carry

    lax.fori_loop(0, chunks, settle, 0)


def per_device(
    n_section,
    n_dp,
    n_mp,
    patches,
    ln_gain,
    ln_bias,
    w_merge_in,
    b_merge_in,
    w_merge_out,
    b_merge_out,
    text_rows,
    section_gain,
    section_weight,
    image_sizes,
    placement,
    offsets,
):
    rows_enc, inner = patches.shape
    depth, features_out = w_merge_out.shape
    seq_len, width = text_rows.shape[2:]
    n_ring = n_mp // 2
    sub = width // n_section
    half = rows_enc // 2
    chunks = n_section * seq_len // ROWS
    per_micro = seq_len // ROWS
    slots = n_section * n_dp * K_PAIR * SLOT
    dma = pltpu.SemaphoreType.DMA
    vmem = pl.BlockSpec(memory_space=pltpu.VMEM)
    hbm = pl.BlockSpec(memory_space=pl.ANY)
    out = pl.pallas_call(
        kernel,
        out_shape=jax.ShapeDtypeStruct((seq_len, width), BF16),
        in_specs=[hbm, vmem, vmem, hbm, vmem, hbm, vmem, vmem, vmem, hbm, vmem, vmem, vmem],
        out_specs=vmem,
        scratch_shapes=[
            pltpu.VMEM((rows_enc, inner), BF16),
            pltpu.VMEM((rows_enc, inner), BF16),
            pltpu.VMEM((depth, inner), BF16),
            pltpu.VMEM((2, n_ring, depth, width), BF16),
            pltpu.VMEM((n_ring, depth, width), BF16),
            pltpu.VMEM((2, rows_enc, depth), BF16),
            pltpu.VMEM((2, 3, PARTS, half, width // PARTS), BF16),
            pltpu.VMEM((2, 3, PARTS, half, width // PARTS), BF16),
            pltpu.VMEM((2, 3, half, sub), BF16),
            pltpu.VMEM((2, 3, half, sub), BF16),
            pltpu.VMEM((2, half, width), F32),
            pltpu.VMEM((rows_enc, sub), BF16),
            pltpu.VMEM((slots, rows_enc), BF16),
            pltpu.VMEM((slots, sub), BF16),
            pltpu.VMEM((n_section, seq_len, width), BF16),
            pltpu.VMEM((seq_len, width), BF16),
            pltpu.VMEM((n_section, seq_len, width), BF16),
            pltpu.VMEM((chunks, 2, n_ring, ROWS, width), BF16),
            pltpu.VMEM((n_mp, width, width), BF16),
            pltpu.VMEM((n_mp, TALL, width), BF16),
            pltpu.VMEM((ROWS, width), F32),
            pltpu.VMEM((ROWS, 128), F32),
            pltpu.VMEM((chunks, ROWS, width), BF16),
            dma((2,)),
            dma((4, n_ring)),
            dma((2,)),
            dma((2, 3, PARTS)),
            dma((2, 3, PARTS)),
            dma((2, 3)),
            dma((2, 3)),
            dma,
            dma((n_section,)),
            dma((n_section, n_dp)),
            dma((chunks,)),
            dma((n_mp,)),
            dma((chunks, 6)),
            dma((chunks, 6)),
            dma((per_micro,)),
        ],
        compiler_params=pltpu.CompilerParams(
            collective_id=0, has_side_effects=True, vmem_limit_bytes=60 * 2**20
        ),
    )(
        patches,
        ln_gain.reshape(-1, 128),
        ln_bias.reshape(-1, 128),
        w_merge_in.T,
        b_merge_in.reshape(1, -1),
        w_merge_out,
        b_merge_out.reshape(-1, 128),
        text_rows.reshape(seq_len, width),
        section_gain,
        section_weight.reshape(n_mp, width, width),
        image_sizes,
        placement,
        offsets,
    )
    return out.reshape(1, 1, seq_len, width)


def solution(mesh):
    in_specs = (
        P("dp", None),
        P(),
        P(),
        P(None, ("section", "mp")),
        P(("section", "mp")),
        P(("section", "mp"), None),
        P(),
        P("section", "dp", None, "mp"),
        P("section", None),
        P("section", None, "mp"),
        P(),
        P(),
        P(),
    )
    out_specs = P("section", "dp", None, "mp")
    sizes = (mesh.shape["section"], mesh.shape["dp"], mesh.shape["mp"])

    def run(*arrays):
        return per_device(*sizes, *arrays)

    return jax.shard_map(run, mesh=mesh, in_specs=in_specs, out_specs=out_specs, check_vma=False)
```

```python
import jax
import jax.numpy as jnp
from jax import lax
from jax.experimental import pallas as pl
from jax.experimental.pallas import tpu as pltpu
from jax.sharding import PartitionSpec as P

SLOT = 8
K_PAIR = 4
ROWS = 32
TALL = 128
LAG = 2
PARTS = 2
MESH = pl.DeviceIdType.MESH
F32 = jnp.float32
BF16 = jnp.bfloat16


def place(slots, sizes, places, starts_at):
    count = sizes.shape[1]
    images = lax.broadcasted_iota(jnp.int32, (slots.shape[0], count), 1)
    match = places == slots // SLOT

    def picked(values):
        return jnp.sum(jnp.where(match, values, 0), axis=1, keepdims=True)

    image = picked(images)
    extent = picked(sizes)
    first = jnp.sum(jnp.where(images < image, sizes, 0), axis=1, keepdims=True)
    column = lax.rem(slots, SLOT) - jnp.minimum(picked(starts_at), SLOT - extent)
    return first + column, (column >= 0) & (column < extent)


def kernel(
    patches_hbm, ln_gain_ref, ln_bias_ref, w_in_hbm, b_in_ref, w_out_hbm, b_out_ref, text_ref,
    gain_ref, weight_hbm, sizes_ref, places_ref, offsets_ref,
    out_ref,
    patches, encoded, w_in, w_out, w_lent, hidden, out1, in1, out2, in2, own, piece, picks, placed, images, text, texts,
    shards, weight, tall, total, squares, results,
    load_sem, w_out_sem, hid_sem, rs1_sent, rs1_got, rs2_sent, rs2_got, text_sent, text_got, place_sent, image_got,
    weight_sem, got, sent, home_sem,
):
    section, dp, mp = (lax.axis_index(a) for a in ("section", "dp", "mp"))
    n_section, n_dp, n_mp = (lax.axis_size(a) for a in ("section", "dp", "mp"))
    n_ring = n_mp // 2
    chip, core = mp // 2, lax.rem(mp, 2)
    chunks, _, _, rows, width = shards.shape
    per_micro = chunks // n_section
    seq_len = rows * per_micro
    per_group = K_PAIR * SLOT
    rows_enc, inner = patches.shape
    features = ln_gain_ref.shape[0] * 128
    half_rows = rows_enc // 2
    sub = width // n_section
    span = width // PARTS

    def at(chip_pos, core_pos):
        return lax.rem(chip_pos + n_ring, n_ring) * 2 + core_pos

    ahead, behind = at(chip + 1, core), at(chip - 1, core)
    sibling = at(chip, 1 - core)
    turn = 1 - 2 * core

    def load(src, dst, slot):
        return pltpu.make_async_copy(src, dst, load_sem.at[slot])

    def load_weight(idx):
        return pltpu.make_async_copy(weight_hbm.at[idx], weight.at[idx], weight_sem.at[idx])

    barrier = pltpu.get_barrier_semaphore()

    def greet(**target):
        pl.semaphore_signal(barrier, inc=1, device_id=target, device_id_type=MESH)

    load(patches_hbm, patches, 1).start()
    load(w_in_hbm, w_in, 0).start()
    for partner in (ahead, behind, sibling):
        greet(mp=partner)

    @pl.when(section == 0)
    def _():
        for there in range(n_section):
            for hop in range(n_dp):
                if there or hop:
                    greet(section=there, dp=lax.rem(dp + hop, n_dp))

    @pl.when(section != 0)
    def _():
        for hop in range(n_dp):
            greet(section=0, dp=lax.rem(dp + hop, n_dp))
        for hop in range(1, n_section):
            there = lax.rem(section + hop, n_section)

            @pl.when(there != 0)
            def _():
                greet(section=there)

    def w_out_block(chip_pos, core_pos):
        columns = pl.multiple_of((chip_pos * 2 + core_pos) * width, width)
        return w_out_hbm.at[:, pl.ds(columns, width)]

    def w_out_own(chip_pos):
        return pltpu.make_async_copy(w_out_block(chip_pos, core), w_out.at[0, chip_pos], w_out_sem.at[0, chip_pos])

    def w_out_fetch(chip_pos):
        return pltpu.make_async_copy(w_out_block(chip_pos, 1 - core), w_lent.at[chip_pos], w_out_sem.at[3, chip_pos])

    def w_out_other(chip_pos):
        return pltpu.make_async_remote_copy(
            src_ref=w_lent.at[chip_pos], dst_ref=w_out.at[1, chip_pos],
            send_sem=w_out_sem.at[1, chip_pos], recv_sem=w_out_sem.at[2, chip_pos],
            device_id={"mp": sibling}, device_id_type=MESH,
        )

    for chip_pos in range(n_ring):
        w_out_fetch(chip_pos).start()
    for chip_pos in range(n_ring):
        w_out_own(chip_pos).start()

    def one_row(ref, begin, count):
        return jnp.concatenate([ref[pl.ds(begin + k, 1), :] for k in range(count)], axis=1)

    ln_gain = one_row(ln_gain_ref, 0, features // 128)
    ln_bias = one_row(ln_bias_ref, 0, features // 128)
    load(patches_hbm, patches, 1).wait()
    block = 16

    def norm(b, carry):
        here = pl.ds(pl.multiple_of(b * block, block), block)
        for q in range(inner // features):
            columns = slice(q * features, (q + 1) * features)
            values = patches[here, columns].astype(F32)
            centre = values - jnp.mean(values, axis=-1, keepdims=True)
            spread = jnp.mean(centre * centre, axis=-1, keepdims=True)
            normed = centre * lax.rsqrt(spread + 1e-06) * ln_gain + ln_bias
            encoded[here, columns] = normed.astype(BF16)
        return carry

    lax.fori_loop(0, rows_enc // block, norm, 0)
    pl.semaphore_wait(barrier, jnp.where(section == 0, n_section * n_dp + 2, n_dp + n_section + 1))

    for chip_pos in range(n_ring):
        w_out_fetch(chip_pos).wait()
        w_out_other(chip_pos).start()

    load(w_in_hbm, w_in, 0).wait()
    before = lax.dot_general(
        encoded[...], w_in[...], (((1,), (1,)), ((), ())), preferred_element_type=F32
    ) + b_in_ref[...]
    hidden[0] = (0.5 * before * (1.0 + lax.erf(before * (0.5**0.5)))).astype(BF16)

    swap = pltpu.make_async_remote_copy(
        src_ref=hidden.at[0], dst_ref=hidden.at[1], send_sem=hid_sem.at[0], recv_sem=hid_sem.at[1],
        device_id={"mp": sibling}, device_id_type=MESH,
    )
    swap.start()
    for chip_pos in range(n_ring):
        w_out_own(chip_pos).wait()
    for chip_pos in range(n_ring):
        w_out_other(chip_pos).wait_recv()
    swap.wait_recv()

    def along(axis, delta):
        if axis:
            return {"section": lax.rem(section + delta + n_section, n_section)}
        return {"mp": at(chip + delta, core)}

    def spot(axis, delta):
        return lax.rem((section if axis else chip) + delta + n_ring, n_ring)

    def partial(h, idx, p):
        def product(k, chip_pos, columns):
            return jnp.dot(
                hidden[k, h * half_rows : (h + 1) * half_rows, :], w_out[k, chip_pos, :, columns],
                preferred_element_type=F32,
            )

        if h == 0:
            columns = slice(p * span, (p + 1) * span)
            return product(0, idx, columns) + product(1, idx, columns)
        columns = pl.ds(pl.multiple_of(idx * sub, sub), sub)
        count = span // sub
        return jnp.concatenate(
            [product(0, z, columns) + product(1, z, columns) for z in range(p * count, (p + 1) * count)], axis=1
        )

    def rs1(h, kind, p, delta):
        return pltpu.make_async_remote_copy(
            src_ref=out1.at[h, kind, p], dst_ref=in1.at[h, kind, p],
            send_sem=rs1_sent.at[h, kind, p], recv_sem=rs1_got.at[h, kind, p],
            device_id=along(h, delta), device_id_type=MESH,
        )

    def rs2(h, kind):
        return pltpu.make_async_remote_copy(
            src_ref=out2.at[h, kind], dst_ref=in2.at[h, kind],
            send_sem=rs2_sent.at[h, kind], recv_sem=rs2_got.at[h, kind],
            device_id=along(1 - h, kind + 1), device_id_type=MESH,
        )

    FAR, NEAR, SUM = 0, 1, 2
    for p in range(PARTS):
        for h in range(2):
            out1[h, FAR, p] = partial(h, spot(h, 2), p).astype(BF16)
            rs1(h, FAR, p, turn).start()
    for p in range(PARTS):
        for h in range(2):
            out1[h, NEAR, p] = partial(h, spot(h, -turn), p).astype(BF16)
            rs1(h, FAR, p, turn).wait_send()
            rs1(h, NEAR, p, -turn).start()
    for p in range(PARTS):
        for h in range(2):
            value = partial(h, spot(h, turn), p)
            rs1(h, FAR, p, turn).wait_recv()
            out1[h, SUM, p] = (value + in1[h, FAR, p].astype(F32)).astype(BF16)
            rs1(h, SUM, p, turn).start()
    for p in range(PARTS):
        for h in range(2):
            own[h, :, p * span : (p + 1) * span] = partial(h, spot(h, 0), p)

    for idx in range(n_mp):
        load_weight(idx).start()

    tall[...] = jnp.zeros_like(tall)

    position = lax.broadcasted_iota(jnp.int32, (seq_len, 1), 0)
    group = position // per_group
    owner = section * n_dp + dp
    slots = owner * per_group + lax.rem(position, per_group)

    def by_group(ref):
        values = jnp.broadcast_to(ref[0:1, :], (seq_len, ref.shape[1]))
        for e in range(1, n_dp):
            values = jnp.where(group == e, ref[e : e + 1, :], values)
        return values

    _, covered = place(slots, by_group(sizes_ref), by_group(places_ref), by_group(offsets_ref))
    text[...] = jnp.where(covered, jnp.zeros((), F32), text_ref[...].astype(F32)).astype(BF16)

    everywhere = lax.broadcasted_iota(jnp.int32, (n_section * n_dp * per_group, 1), 0)
    mine = pl.ds(dp, 1)
    row, covered = place(everywhere, sizes_ref[mine, :], places_ref[mine, :], offsets_ref[mine, :])
    candidates = lax.broadcasted_iota(jnp.int32, (everywhere.shape[0], rows_enc), 1)
    picks[...] = jnp.where((candidates == row) & covered, 1.0, 0.0).astype(BF16)

    for p in range(PARTS):
        for h in range(2):
            columns = slice(p * span, (p + 1) * span)
            rs1(h, NEAR, p, -turn).wait_recv()
            rs1(h, SUM, p, turn).wait_recv()
            own[h, :, columns] += in1[h, NEAR, p].astype(F32) + in1[h, SUM, p].astype(F32)

    def own_block(h, delta):
        columns = pl.ds(pl.multiple_of(spot(1 - h, delta) * sub, sub), sub)
        return own[h, :, columns]

    for kind in (1, 0, 2):
        for h in range(2):
            out2[h, kind] = own_block(h, kind + 1).astype(BF16)
            rs2(h, kind).start()
    bias = one_row(b_out_ref, (mp * n_section + section) * (sub // 128), sub // 128)
    for h in range(2):
        value = own_block(h, 0) + bias
        for kind in (0, 2, 1):
            rs2(h, kind).wait_recv()
            value = value + in2[h, kind].astype(F32)
        piece[h * half_rows : (h + 1) * half_rows, :] = value.astype(BF16)

    placed[...] = jnp.dot(picks[...], piece[...], preferred_element_type=F32).astype(BF16)

    def block_of(micro, seq):
        begin = pl.multiple_of((micro * n_dp + seq) * per_group, per_group)
        return placed.at[pl.ds(begin, per_group)]

    def landing(micro):
        return images.at[
            micro, pl.ds(pl.multiple_of(dp * per_group, per_group), per_group),
            pl.ds(pl.multiple_of(section * sub, sub), sub),
        ]

    part_of = dp * per_group // rows

    def deliver(micro, hop):
        seq = lax.rem(dp + hop, n_dp)
        return pltpu.make_async_remote_copy(
            src_ref=block_of(micro, seq), dst_ref=landing(micro),
            send_sem=place_sent.at[micro, hop], recv_sem=image_got.at[micro * per_micro + part_of],
            device_id={"section": 0, "dp": seq}, device_id_type=MESH,
        )

    def feed():
        return pltpu.make_async_remote_copy(
            src_ref=text, dst_ref=texts.at[section],
            send_sem=text_sent, recv_sem=text_got.at[section],
            device_id={"section": 0}, device_id_type=MESH,
        )

    def keep(micro):
        pltpu.make_async_copy(
            block_of(micro, dp), landing(micro), image_got.at[micro * per_micro + part_of]
        ).start()

    def deliver_all(micro):
        for hop in range(n_dp):
            deliver(micro, hop).start()

    def delivered(micro):
        for hop in range(n_dp):
            deliver(micro, hop).wait_send()

    paced = 2

    @pl.when(section == 0)
    def _():
        pltpu.make_async_copy(text, texts.at[0], text_got.at[0]).start()
        keep(0)
        for hop in range(1, n_dp):
            deliver(0, hop).start()

    @pl.when(section != 0)
    def _():
        for micro in range(n_section):
            if micro:
                @pl.when(section == micro)
                def _():
                    feed().start()

            deliver_all(micro)
            if micro < paced:
                delivered(micro)

    def ring(step):
        return lax.rem(chip + step * turn + n_ring, n_ring)

    def shard_copy(t, step, slot):
        return pltpu.make_async_remote_copy(
            src_ref=shards.at[t, core, chip], dst_ref=shards.at[t, core, chip],
            send_sem=sent.at[t, slot], recv_sem=got.at[t, slot],
            device_id={"mp": at(chip + step * turn, core)}, device_id_type=MESH,
        )

    def entry(t):
        return pltpu.make_async_remote_copy(
            src_ref=results.at[t], dst_ref=shards.at[t, core, chip],
            send_sem=sent.at[t, 4], recv_sem=got.at[t, 4],
            device_id={"section": lax.rem(section + 1, n_section)}, device_id_type=MESH,
        )

    def lend(t):
        return pltpu.make_async_remote_copy(
            src_ref=shards.at[t, core], dst_ref=shards.at[t, core],
            send_sem=sent.at[t, 3], recv_sem=got.at[t, 3],
            device_id={"mp": sibling}, device_id_type=MESH,
        )

    def enter(t):
        micro, part = t // per_micro, lax.rem(t, per_micro)
        here = pl.ds(pl.multiple_of(part * rows, rows), rows)

        @pl.when(part == 0)
        def _():
            pltpu.make_async_remote_copy(
                src_ref=text, dst_ref=texts.at[micro], send_sem=text_sent, recv_sem=text_got.at[micro],
                device_id={"section": 0}, device_id_type=MESH,
            ).wait_recv()

        pltpu.make_async_remote_copy(
            src_ref=images.at[micro, here], dst_ref=images.at[micro, here],
            send_sem=text_sent, recv_sem=image_got.at[t],
            device_id={"section": 0}, device_id_type=MESH,
        ).wait_recv()
        shards[t, core, chip] = (images[micro, here, :].astype(F32) + texts[micro, here, :].astype(F32)).astype(BF16)

    def bring_home(t):
        half = lax.rem(t, per_micro)
        return pltpu.make_async_remote_copy(
            src_ref=results.at[t], dst_ref=out_ref.at[pl.ds(pl.multiple_of(half * rows, rows), rows)],
            send_sem=sent.at[t, 4], recv_sem=home_sem.at[half],
            device_id={"section": t // per_micro}, device_id_type=MESH,
        )

    def add(t, core_pos, chip_pos, spare):
        first = spare == 0
        idx = chip_pos * 2 + core_pos
        values = shards[t, core_pos, chip_pos].astype(F32)
        square = values * values
        lanes = square[:, :128] if first else squares[...] + square[:, :128]
        for j in range(128, width, 128):
            lanes = lanes + square[:, j : j + 128]
        squares[...] = lanes
        gain = gain_ref[:, pl.ds(pl.multiple_of(idx * width, width), width)]
        tall[spare, 0:rows] = (values * gain).astype(BF16)
        update = jnp.dot(tall[spare], weight[idx], preferred_element_type=F32)[0:rows]
        total[...] = update if first else total[...] + update

    last = n_section - 1
    def begin(t):
        @pl.when(section == 0)
        def _():
            enter(t)

        @pl.when(section != 0)
        def _():
            entry(t).wait_recv()

        shard_copy(t, 2, 2).start()
        shard_copy(t, 1, 0).start()
        shard_copy(t, -1, 1).start()

    def share(t):
        for slot in range(3):
            shard_copy(t, 1, slot).wait_recv()
        lend(t).start()

    def multiply(t):
        for step in range(n_ring):
            add(t, core, ring(step), step)
        lend(t).wait_recv()
        for step in range(n_ring):
            add(t, 1 - core, ring(step), n_ring + step)
        square = jnp.sum(squares[...], axis=-1, keepdims=True) * (1.0 / (n_mp * width))
        update = total[...] * lax.rsqrt(square + 1e-06)
        result = (shards[t, core, chip].astype(F32) + update).astype(BF16)
        results[t] = result

        @pl.when(section < last)
        def _():
            entry(t).start()

        @pl.when((section == last) & (t < last * per_micro))
        def _():
            bring_home(t).start()

        @pl.when((section == last) & (t >= last * per_micro))
        def _():
            part = lax.rem(t, per_micro)
            out_ref[pl.ds(pl.multiple_of(part * rows, rows), rows)] = result

    def turn_body(i, carry):
        @pl.when(i < chunks)
        def _():
            begin(i)

        @pl.when((i == 1) & (section == 0))
        def _():
            for micro in range(1, n_section):
                keep(micro)
                for hop in range(1, n_dp):
                    deliver(micro, hop).start()

        @pl.when(i == LAG)
        def _():
            for idx in range(n_mp):
                load_weight(idx).wait()

        t = i - LAG

        @pl.when(t >= 0)
        def _():
            multiply(t)

        @pl.when((i >= LAG - 1) & (i < chunks + LAG - 1))
        def _():
            share(t + 1)

        return carry

    lax.fori_loop(0, chunks + LAG, turn_body, 0)

    @pl.when(section < last)
    def _():
        for half in range(per_micro):
            bring_home(half).wait_recv()

    for chip_pos in range(n_ring):
        w_out_other(chip_pos).wait_send()
    swap.wait_send()
    for h in range(2):
        for kind in range(3):
            if kind != FAR:
                for p in range(PARTS):
                    rs1(h, kind, p, 1).wait_send()
            rs2(h, kind).wait_send()

    @pl.when(section == 0)
    def _():
        for micro in range(n_section):
            for hop in range(1, n_dp):
                deliver(micro, hop).wait_send()

    @pl.when(section != 0)
    def _():
        feed().wait_send()
        for micro in range(paced, n_section):
            delivered(micro)

    def settle(t, carry):
        for slot in range(3):
            shard_copy(t, 1, slot).wait_send()
        lend(t).wait_send()

        @pl.when((section < last) | (t < last * per_micro))
        def _():
            entry(t).wait_send()

        return carry

    lax.fori_loop(0, chunks, settle, 0)


def per_device(
    n_section,
    n_dp,
    n_mp,
    patches,
    ln_gain,
    ln_bias,
    w_merge_in,
    b_merge_in,
    w_merge_out,
    b_merge_out,
    text_rows,
    section_gain,
    section_weight,
    image_sizes,
    placement,
    offsets,
):
    rows_enc, inner = patches.shape
    depth, features_out = w_merge_out.shape
    seq_len, width = text_rows.shape[2:]
    n_ring = n_mp // 2
    sub = width // n_section
    half = rows_enc // 2
    chunks = n_section * seq_len // ROWS
    per_micro = seq_len // ROWS
    slots = n_section * n_dp * K_PAIR * SLOT
    dma = pltpu.SemaphoreType.DMA
    vmem = pl.BlockSpec(memory_space=pltpu.VMEM)
    hbm = pl.BlockSpec(memory_space=pl.ANY)
    out = pl.pallas_call(
        kernel,
        out_shape=jax.ShapeDtypeStruct((seq_len, width), BF16),
        in_specs=[hbm, vmem, vmem, hbm, vmem, hbm, vmem, vmem, vmem, hbm, vmem, vmem, vmem],
        out_specs=vmem,
        scratch_shapes=[
            pltpu.VMEM((rows_enc, inner), BF16),
            pltpu.VMEM((rows_enc, inner), BF16),
            pltpu.VMEM((depth, inner), BF16),
            pltpu.VMEM((2, n_ring, depth, width), BF16),
            pltpu.VMEM((n_ring, depth, width), BF16),
            pltpu.VMEM((2, rows_enc, depth), BF16),
            pltpu.VMEM((2, 3, PARTS, half, width // PARTS), BF16),
            pltpu.VMEM((2, 3, PARTS, half, width // PARTS), BF16),
            pltpu.VMEM((2, 3, half, sub), BF16),
            pltpu.VMEM((2, 3, half, sub), BF16),
            pltpu.VMEM((2, half, width), F32),
            pltpu.VMEM((rows_enc, sub), BF16),
            pltpu.VMEM((slots, rows_enc), BF16),
            pltpu.VMEM((slots, sub), BF16),
            pltpu.VMEM((n_section, seq_len, width), BF16),
            pltpu.VMEM((seq_len, width), BF16),
            pltpu.VMEM((n_section, seq_len, width), BF16),
            pltpu.VMEM((chunks, 2, n_ring, ROWS, width), BF16),
            pltpu.VMEM((n_mp, width, width), BF16),
            pltpu.VMEM((n_mp, TALL, width), BF16),
            pltpu.VMEM((ROWS, width), F32),
            pltpu.VMEM((ROWS, 128), F32),
            pltpu.VMEM((chunks, ROWS, width), BF16),
            dma((2,)),
            dma((4, n_ring)),
            dma((2,)),
            dma((2, 3, PARTS)),
            dma((2, 3, PARTS)),
            dma((2, 3)),
            dma((2, 3)),
            dma,
            dma((n_section,)),
            dma((n_section, n_dp)),
            dma((chunks,)),
            dma((n_mp,)),
            dma((chunks, 5)),
            dma((chunks, 5)),
            dma((per_micro,)),
        ],
        compiler_params=pltpu.CompilerParams(
            collective_id=0, has_side_effects=True, vmem_limit_bytes=60 * 2**20
        ),
    )(
        patches,
        ln_gain.reshape(-1, 128),
        ln_bias.reshape(-1, 128),
        w_merge_in.T,
        b_merge_in.reshape(1, -1),
        w_merge_out,
        b_merge_out.reshape(-1, 128),
        text_rows.reshape(seq_len, width),
        section_gain,
        section_weight.reshape(n_mp, width, width),
        image_sizes,
        placement,
        offsets,
    )
    return out.reshape(1, 1, seq_len, width)


def solution(mesh):
    in_specs = (
        P("dp", None),
        P(),
        P(),
        P(None, ("section", "mp")),
        P(("section", "mp")),
        P(("section", "mp"), None),
        P(),
        P("section", "dp", None, "mp"),
        P("section", None),
        P("section", None, "mp"),
        P(),
        P(),
        P(),
    )
    out_specs = P("section", "dp", None, "mp")
    sizes = (mesh.shape["section"], mesh.shape["dp"], mesh.shape["mp"])

    def run(*arrays):
        return per_device(*sizes, *arrays)

    return jax.shard_map(run, mesh=mesh, in_specs=in_specs, out_specs=out_specs, check_vma=False)
```

```python
import jax
import jax.numpy as jnp
from jax import lax
from jax.experimental import pallas as pl
from jax.experimental.pallas import tpu as pltpu
from jax.sharding import PartitionSpec as P

SLOT = 8
K_PAIR = 4
ROWS = 32
TALL = 128
LAG = 2
PARTS = 2
MESH = pl.DeviceIdType.MESH
F32 = jnp.float32
BF16 = jnp.bfloat16


def place(slots, sizes, places, starts_at):
    count = sizes.shape[1]
    images = lax.broadcasted_iota(jnp.int32, (slots.shape[0], count), 1)
    match = places == slots // SLOT

    def picked(values):
        return jnp.sum(jnp.where(match, values, 0), axis=1, keepdims=True)

    image = picked(images)
    extent = picked(sizes)
    first = jnp.sum(jnp.where(images < image, sizes, 0), axis=1, keepdims=True)
    column = lax.rem(slots, SLOT) - jnp.minimum(picked(starts_at), SLOT - extent)
    return first + column, (column >= 0) & (column < extent)


def kernel(
    patches_hbm, ln_gain_ref, ln_bias_ref, w_in_hbm, b_in_ref, w_out_hbm, b_out_ref, text_ref,
    gain_ref, weight_hbm, sizes_ref, places_ref, offsets_ref,
    out_ref,
    patches, encoded, w_in, w_out, w_lent, hidden, out1, in1, out2, in2, own, piece, picks, placed, images, text, texts,
    shards, weight, tall, total, squares, results,
    load_sem, w_out_sem, hid_sem, rs1_sent, rs1_got, rs2_sent, rs2_got, text_sent, text_got, place_sent, image_got,
    weight_sem, got, sent, home_sem,
):
    section, dp, mp = (lax.axis_index(a) for a in ("section", "dp", "mp"))
    n_section, n_dp, n_mp = (lax.axis_size(a) for a in ("section", "dp", "mp"))
    n_ring = n_mp // 2
    chip, core = mp // 2, lax.rem(mp, 2)
    chunks, _, _, rows, width = shards.shape
    per_micro = chunks // n_section
    seq_len = rows * per_micro
    per_group = K_PAIR * SLOT
    rows_enc, inner = patches.shape
    features = ln_gain_ref.shape[0] * 128
    half_rows = rows_enc // 2
    sub = width // n_section
    span = width // PARTS

    def at(chip_pos, core_pos):
        return lax.rem(chip_pos + n_ring, n_ring) * 2 + core_pos

    ahead, behind = at(chip + 1, core), at(chip - 1, core)
    sibling = at(chip, 1 - core)
    turn = 1 - 2 * core

    def load(src, dst, slot):
        return pltpu.make_async_copy(src, dst, load_sem.at[slot])

    def load_weight(idx):
        return pltpu.make_async_copy(weight_hbm.at[idx], weight.at[idx], weight_sem.at[idx])

    barrier = pltpu.get_barrier_semaphore()

    def greet(**target):
        pl.semaphore_signal(barrier, inc=1, device_id=target, device_id_type=MESH)

    load(patches_hbm, patches, 1).start()
    load(w_in_hbm, w_in, 0).start()
    for partner in (ahead, behind, sibling):
        greet(mp=partner)

    @pl.when(section == 0)
    def _():
        for there in range(n_section):
            for hop in range(n_dp):
                if there or hop:
                    greet(section=there, dp=lax.rem(dp + hop, n_dp))

    @pl.when(section != 0)
    def _():
        for hop in range(n_dp):
            greet(section=0, dp=lax.rem(dp + hop, n_dp))
        for hop in range(1, n_section):
            there = lax.rem(section + hop, n_section)

            @pl.when(there != 0)
            def _():
                greet(section=there)

    def w_out_block(chip_pos, core_pos):
        columns = pl.multiple_of((chip_pos * 2 + core_pos) * width, width)
        return w_out_hbm.at[:, pl.ds(columns, width)]

    def w_out_own(chip_pos):
        return pltpu.make_async_copy(w_out_block(chip_pos, core), w_out.at[0, chip_pos], w_out_sem.at[0, chip_pos])

    def w_out_fetch(chip_pos):
        return pltpu.make_async_copy(w_out_block(chip_pos, 1 - core), w_lent.at[chip_pos], w_out_sem.at[3, chip_pos])

    def w_out_other(chip_pos):
        return pltpu.make_async_remote_copy(
            src_ref=w_lent.at[chip_pos], dst_ref=w_out.at[1, chip_pos],
            send_sem=w_out_sem.at[1, chip_pos], recv_sem=w_out_sem.at[2, chip_pos],
            device_id={"mp": sibling}, device_id_type=MESH,
        )

    for chip_pos in range(n_ring):
        w_out_fetch(chip_pos).start()
    for chip_pos in range(n_ring):
        w_out_own(chip_pos).start()

    def one_row(ref, begin, count):
        return jnp.concatenate([ref[pl.ds(begin + k, 1), :] for k in range(count)], axis=1)

    ln_gain = one_row(ln_gain_ref, 0, features // 128)
    ln_bias = one_row(ln_bias_ref, 0, features // 128)
    load(patches_hbm, patches, 1).wait()
    block = 16

    def norm(b, carry):
        here = pl.ds(pl.multiple_of(b * block, block), block)
        for q in range(inner // features):
            columns = slice(q * features, (q + 1) * features)
            values = patches[here, columns].astype(F32)
            centre = values - jnp.mean(values, axis=-1, keepdims=True)
            spread = jnp.mean(centre * centre, axis=-1, keepdims=True)
            normed = centre * lax.rsqrt(spread + 1e-06) * ln_gain + ln_bias
            encoded[here, columns] = normed.astype(BF16)
        return carry

    lax.fori_loop(0, rows_enc // block, norm, 0)
    load(w_in_hbm, w_in, 0).wait()
    before = lax.dot_general(
        encoded[...], w_in[...], (((1,), (1,)), ((), ())), preferred_element_type=F32
    ) + b_in_ref[...]
    hidden[0] = (0.5 * before * (1.0 + lax.erf(before * (0.5**0.5)))).astype(BF16)

    pl.semaphore_wait(barrier, jnp.where(section == 0, n_section * n_dp + 2, n_dp + n_section + 1))

    for chip_pos in range(n_ring):
        w_out_fetch(chip_pos).wait()
        w_out_other(chip_pos).start()

    swap = pltpu.make_async_remote_copy(
        src_ref=hidden.at[0], dst_ref=hidden.at[1], send_sem=hid_sem.at[0], recv_sem=hid_sem.at[1],
        device_id={"mp": sibling}, device_id_type=MESH,
    )
    swap.start()
    for chip_pos in range(n_ring):
        w_out_own(chip_pos).wait()
    for chip_pos in range(n_ring):
        w_out_other(chip_pos).wait_recv()
    swap.wait_recv()

    def along(axis, delta):
        if axis:
            return {"section": lax.rem(section + delta + n_section, n_section)}
        return {"mp": at(chip + delta, core)}

    def spot(axis, delta):
        return lax.rem((section if axis else chip) + delta + n_ring, n_ring)

    def partial(h, idx, p):
        def product(k, chip_pos, columns):
            return jnp.dot(
                hidden[k, h * half_rows : (h + 1) * half_rows, :], w_out[k, chip_pos, :, columns],
                preferred_element_type=F32,
            )

        if h == 0:
            columns = slice(p * span, (p + 1) * span)
            return product(0, idx, columns) + product(1, idx, columns)
        columns = pl.ds(pl.multiple_of(idx * sub, sub), sub)
        count = span // sub
        return jnp.concatenate(
            [product(0, z, columns) + product(1, z, columns) for z in range(p * count, (p + 1) * count)], axis=1
        )

    def rs1(h, kind, p, delta):
        return pltpu.make_async_remote_copy(
            src_ref=out1.at[h, kind, p], dst_ref=in1.at[h, kind, p],
            send_sem=rs1_sent.at[h, kind, p], recv_sem=rs1_got.at[h, kind, p],
            device_id=along(h, delta), device_id_type=MESH,
        )

    def rs2(h, kind):
        return pltpu.make_async_remote_copy(
            src_ref=out2.at[h, kind], dst_ref=in2.at[h, kind],
            send_sem=rs2_sent.at[h, kind], recv_sem=rs2_got.at[h, kind],
            device_id=along(1 - h, kind + 1), device_id_type=MESH,
        )

    FAR, NEAR, SUM = 0, 1, 2
    for p in range(PARTS):
        for h in range(2):
            out1[h, FAR, p] = partial(h, spot(h, 2), p).astype(BF16)
            rs1(h, FAR, p, turn).start()
    for p in range(PARTS):
        for h in range(2):
            out1[h, NEAR, p] = partial(h, spot(h, -turn), p).astype(BF16)
            rs1(h, FAR, p, turn).wait_send()
            rs1(h, NEAR, p, -turn).start()
    for p in range(PARTS):
        for h in range(2):
            value = partial(h, spot(h, turn), p)
            rs1(h, FAR, p, turn).wait_recv()
            out1[h, SUM, p] = (value + in1[h, FAR, p].astype(F32)).astype(BF16)
            rs1(h, SUM, p, turn).start()
    for p in range(PARTS):
        for h in range(2):
            own[h, :, p * span : (p + 1) * span] = partial(h, spot(h, 0), p)

    for idx in range(n_mp):
        load_weight(idx).start()

    tall[...] = jnp.zeros_like(tall)

    position = lax.broadcasted_iota(jnp.int32, (seq_len, 1), 0)
    group = position // per_group
    owner = section * n_dp + dp
    slots = owner * per_group + lax.rem(position, per_group)

    def by_group(ref):
        values = jnp.broadcast_to(ref[0:1, :], (seq_len, ref.shape[1]))
        for e in range(1, n_dp):
            values = jnp.where(group == e, ref[e : e + 1, :], values)
        return values

    _, covered = place(slots, by_group(sizes_ref), by_group(places_ref), by_group(offsets_ref))
    text[...] = jnp.where(covered, jnp.zeros((), F32), text_ref[...].astype(F32)).astype(BF16)

    everywhere = lax.broadcasted_iota(jnp.int32, (n_section * n_dp * per_group, 1), 0)
    mine = pl.ds(dp, 1)
    row, covered = place(everywhere, sizes_ref[mine, :], places_ref[mine, :], offsets_ref[mine, :])
    candidates = lax.broadcasted_iota(jnp.int32, (everywhere.shape[0], rows_enc), 1)
    picks[...] = jnp.where((candidates == row) & covered, 1.0, 0.0).astype(BF16)

    for p in range(PARTS):
        for h in range(2):
            columns = slice(p * span, (p + 1) * span)
            rs1(h, NEAR, p, -turn).wait_recv()
            rs1(h, SUM, p, turn).wait_recv()
            own[h, :, columns] += in1[h, NEAR, p].astype(F32) + in1[h, SUM, p].astype(F32)

    def own_block(h, delta):
        columns = pl.ds(pl.multiple_of(spot(1 - h, delta) * sub, sub), sub)
        return own[h, :, columns]

    for kind in (1, 0, 2):
        for h in range(2):
            out2[h, kind] = own_block(h, kind + 1).astype(BF16)
            rs2(h, kind).start()
    bias = one_row(b_out_ref, (mp * n_section + section) * (sub // 128), sub // 128)
    for h in range(2):
        value = own_block(h, 0) + bias
        for kind in (0, 2, 1):
            rs2(h, kind).wait_recv()
            value = value + in2[h, kind].astype(F32)
        piece[h * half_rows : (h + 1) * half_rows, :] = value.astype(BF16)

    placed[...] = jnp.dot(picks[...], piece[...], preferred_element_type=F32).astype(BF16)

    def block_of(micro, seq):
        begin = pl.multiple_of((micro * n_dp + seq) * per_group, per_group)
        return placed.at[pl.ds(begin, per_group)]

    def landing(micro):
        return images.at[
            micro, pl.ds(pl.multiple_of(dp * per_group, per_group), per_group),
            pl.ds(pl.multiple_of(section * sub, sub), sub),
        ]

    part_of = dp * per_group // rows

    def deliver(micro, hop):
        seq = lax.rem(dp + hop, n_dp)
        return pltpu.make_async_remote_copy(
            src_ref=block_of(micro, seq), dst_ref=landing(micro),
            send_sem=place_sent.at[micro, hop], recv_sem=image_got.at[micro * per_micro + part_of],
            device_id={"section": 0, "dp": seq}, device_id_type=MESH,
        )

    def feed():
        return pltpu.make_async_remote_copy(
            src_ref=text, dst_ref=texts.at[section],
            send_sem=text_sent, recv_sem=text_got.at[section],
            device_id={"section": 0}, device_id_type=MESH,
        )

    def keep(micro):
        pltpu.make_async_copy(
            block_of(micro, dp), landing(micro), image_got.at[micro * per_micro + part_of]
        ).start()

    def deliver_all(micro):
        for hop in range(n_dp):
            deliver(micro, hop).start()

    def delivered(micro):
        for hop in range(n_dp):
            deliver(micro, hop).wait_send()

    paced = 2

    @pl.when(section == 0)
    def _():
        pltpu.make_async_copy(text, texts.at[0], text_got.at[0]).start()
        keep(0)
        for hop in range(1, n_dp):
            deliver(0, hop).start()

    @pl.when(section != 0)
    def _():
        for micro in range(n_section):
            if micro:
                @pl.when(section == micro)
                def _():
                    feed().start()

            deliver_all(micro)
            if micro < paced:
                delivered(micro)

    def ring(step):
        return lax.rem(chip + step * turn + n_ring, n_ring)

    def shard_copy(t, step, slot):
        return pltpu.make_async_remote_copy(
            src_ref=shards.at[t, core, chip], dst_ref=shards.at[t, core, chip],
            send_sem=sent.at[t, slot], recv_sem=got.at[t, slot],
            device_id={"mp": at(chip + step * turn, core)}, device_id_type=MESH,
        )

    def entry(t):
        return pltpu.make_async_remote_copy(
            src_ref=results.at[t], dst_ref=shards.at[t, core, chip],
            send_sem=sent.at[t, 4], recv_sem=got.at[t, 4],
            device_id={"section": lax.rem(section + 1, n_section)}, device_id_type=MESH,
        )

    def lend(t):
        return pltpu.make_async_remote_copy(
            src_ref=shards.at[t, core], dst_ref=shards.at[t, core],
            send_sem=sent.at[t, 3], recv_sem=got.at[t, 3],
            device_id={"mp": sibling}, device_id_type=MESH,
        )

    def enter(t):
        micro, part = t // per_micro, lax.rem(t, per_micro)
        here = pl.ds(pl.multiple_of(part * rows, rows), rows)

        @pl.when(part == 0)
        def _():
            pltpu.make_async_remote_copy(
                src_ref=text, dst_ref=texts.at[micro], send_sem=text_sent, recv_sem=text_got.at[micro],
                device_id={"section": 0}, device_id_type=MESH,
            ).wait_recv()

        pltpu.make_async_remote_copy(
            src_ref=images.at[micro, here], dst_ref=images.at[micro, here],
            send_sem=text_sent, recv_sem=image_got.at[t],
            device_id={"section": 0}, device_id_type=MESH,
        ).wait_recv()
        shards[t, core, chip] = (images[micro, here, :].astype(F32) + texts[micro, here, :].astype(F32)).astype(BF16)

    def bring_home(t):
        half = lax.rem(t, per_micro)
        return pltpu.make_async_remote_copy(
            src_ref=results.at[t], dst_ref=out_ref.at[pl.ds(pl.multiple_of(half * rows, rows), rows)],
            send_sem=sent.at[t, 4], recv_sem=home_sem.at[half],
            device_id={"section": t // per_micro}, device_id_type=MESH,
        )

    def add(t, core_pos, chip_pos, spare):
        first = spare == 0
        idx = chip_pos * 2 + core_pos
        values = shards[t, core_pos, chip_pos].astype(F32)
        square = values * values
        lanes = square[:, :128] if first else squares[...] + square[:, :128]
        for j in range(128, width, 128):
            lanes = lanes + square[:, j : j + 128]
        squares[...] = lanes
        gain = gain_ref[:, pl.ds(pl.multiple_of(idx * width, width), width)]
        tall[spare, 0:rows] = (values * gain).astype(BF16)
        update = jnp.dot(tall[spare], weight[idx], preferred_element_type=F32)[0:rows]
        total[...] = update if first else total[...] + update

    last = n_section - 1
    def begin(t):
        @pl.when(section == 0)
        def _():
            enter(t)

        @pl.when(section != 0)
        def _():
            entry(t).wait_recv()

        shard_copy(t, 2, 2).start()
        shard_copy(t, 1, 0).start()
        shard_copy(t, -1, 1).start()

    def share(t):
        for slot in range(3):
            shard_copy(t, 1, slot).wait_recv()
        lend(t).start()

    def multiply(t):
        for step in range(n_ring):
            add(t, core, ring(step), step)
        lend(t).wait_recv()
        for step in range(n_ring):
            add(t, 1 - core, ring(step), n_ring + step)
        square = jnp.sum(squares[...], axis=-1, keepdims=True) * (1.0 / (n_mp * width))
        update = total[...] * lax.rsqrt(square + 1e-06)
        result = (shards[t, core, chip].astype(F32) + update).astype(BF16)
        results[t] = result

        @pl.when(section < last)
        def _():
            entry(t).start()

        @pl.when((section == last) & (t < last * per_micro))
        def _():
            bring_home(t).start()

        @pl.when((section == last) & (t >= last * per_micro))
        def _():
            part = lax.rem(t, per_micro)
            out_ref[pl.ds(pl.multiple_of(part * rows, rows), rows)] = result

    def turn_body(i, carry):
        @pl.when(i < chunks)
        def _():
            begin(i)

        @pl.when((i == 1) & (section == 0))
        def _():
            for micro in range(1, n_section):
                keep(micro)
                for hop in range(1, n_dp):
                    deliver(micro, hop).start()

        @pl.when(i == LAG)
        def _():
            for idx in range(n_mp):
                load_weight(idx).wait()

        t = i - LAG

        @pl.when(t >= 0)
        def _():
            share(t)
            multiply(t)

        return carry

    lax.fori_loop(0, chunks + LAG, turn_body, 0)

    @pl.when(section < last)
    def _():
        for half in range(per_micro):
            bring_home(half).wait_recv()

    for chip_pos in range(n_ring):
        w_out_other(chip_pos).wait_send()
    swap.wait_send()
    for h in range(2):
        for kind in range(3):
            if kind != FAR:
                for p in range(PARTS):
                    rs1(h, kind, p, 1).wait_send()
            rs2(h, kind).wait_send()

    @pl.when(section == 0)
    def _():
        for micro in range(n_section):
            for hop in range(1, n_dp):
                deliver(micro, hop).wait_send()

    @pl.when(section != 0)
    def _():
        feed().wait_send()
        for micro in range(paced, n_section):
            delivered(micro)

    def settle(t, carry):
        for slot in range(3):
            shard_copy(t, 1, slot).wait_send()
        lend(t).wait_send()

        @pl.when((section < last) | (t < last * per_micro))
        def _():
            entry(t).wait_send()

        return carry

    lax.fori_loop(0, chunks, settle, 0)


def per_device(
    n_section,
    n_dp,
    n_mp,
    patches,
    ln_gain,
    ln_bias,
    w_merge_in,
    b_merge_in,
    w_merge_out,
    b_merge_out,
    text_rows,
    section_gain,
    section_weight,
    image_sizes,
    placement,
    offsets,
):
    rows_enc, inner = patches.shape
    depth, features_out = w_merge_out.shape
    seq_len, width = text_rows.shape[2:]
    n_ring = n_mp // 2
    sub = width // n_section
    half = rows_enc // 2
    chunks = n_section * seq_len // ROWS
    per_micro = seq_len // ROWS
    slots = n_section * n_dp * K_PAIR * SLOT
    dma = pltpu.SemaphoreType.DMA
    vmem = pl.BlockSpec(memory_space=pltpu.VMEM)
    hbm = pl.BlockSpec(memory_space=pl.ANY)
    out = pl.pallas_call(
        kernel,
        out_shape=jax.ShapeDtypeStruct((seq_len, width), BF16),
        in_specs=[hbm, vmem, vmem, hbm, vmem, hbm, vmem, vmem, vmem, hbm, vmem, vmem, vmem],
        out_specs=vmem,
        scratch_shapes=[
            pltpu.VMEM((rows_enc, inner), BF16),
            pltpu.VMEM((rows_enc, inner), BF16),
            pltpu.VMEM((depth, inner), BF16),
            pltpu.VMEM((2, n_ring, depth, width), BF16),
            pltpu.VMEM((n_ring, depth, width), BF16),
            pltpu.VMEM((2, rows_enc, depth), BF16),
            pltpu.VMEM((2, 3, PARTS, half, width // PARTS), BF16),
            pltpu.VMEM((2, 3, PARTS, half, width // PARTS), BF16),
            pltpu.VMEM((2, 3, half, sub), BF16),
            pltpu.VMEM((2, 3, half, sub), BF16),
            pltpu.VMEM((2, half, width), F32),
            pltpu.VMEM((rows_enc, sub), BF16),
            pltpu.VMEM((slots, rows_enc), BF16),
            pltpu.VMEM((slots, sub), BF16),
            pltpu.VMEM((n_section, seq_len, width), BF16),
            pltpu.VMEM((seq_len, width), BF16),
            pltpu.VMEM((n_section, seq_len, width), BF16),
            pltpu.VMEM((chunks, 2, n_ring, ROWS, width), BF16),
            pltpu.VMEM((n_mp, width, width), BF16),
            pltpu.VMEM((n_mp, TALL, width), BF16),
            pltpu.VMEM((ROWS, width), F32),
            pltpu.VMEM((ROWS, 128), F32),
            pltpu.VMEM((chunks, ROWS, width), BF16),
            dma((2,)),
            dma((4, n_ring)),
            dma((2,)),
            dma((2, 3, PARTS)),
            dma((2, 3, PARTS)),
            dma((2, 3)),
            dma((2, 3)),
            dma,
            dma((n_section,)),
            dma((n_section, n_dp)),
            dma((chunks,)),
            dma((n_mp,)),
            dma((chunks, 5)),
            dma((chunks, 5)),
            dma((per_micro,)),
        ],
        compiler_params=pltpu.CompilerParams(
            collective_id=0, has_side_effects=True, vmem_limit_bytes=60 * 2**20
        ),
    )(
        patches,
        ln_gain.reshape(-1, 128),
        ln_bias.reshape(-1, 128),
        w_merge_in.T,
        b_merge_in.reshape(1, -1),
        w_merge_out,
        b_merge_out.reshape(-1, 128),
        text_rows.reshape(seq_len, width),
        section_gain,
        section_weight.reshape(n_mp, width, width),
        image_sizes,
        placement,
        offsets,
    )
    return out.reshape(1, 1, seq_len, width)


def solution(mesh):
    in_specs = (
        P("dp", None),
        P(),
        P(),
        P(None, ("section", "mp")),
        P(("section", "mp")),
        P(("section", "mp"), None),
        P(),
        P("section", "dp", None, "mp"),
        P("section", None),
        P("section", None, "mp"),
        P(),
        P(),
        P(),
    )
    out_specs = P("section", "dp", None, "mp")
    sizes = (mesh.shape["section"], mesh.shape["dp"], mesh.shape["mp"])

    def run(*arrays):
        return per_device(*sizes, *arrays)

    return jax.shard_map(run, mesh=mesh, in_specs=in_specs, out_specs=out_specs, check_vma=False)
```
